32 devices in a mesh: ctx: 8 (over y, x, core), dp: 4 (over z).
Axes of the slice: x: 2, y: 2, z: 4, core: 2. Of those that a mesh axis runs over, the one named last changes fastest.
Arguments:
- queries: bfloat16 [4, 2048, 1024], P('dp', 'ctx'), may hold values from -6 to 6
- key_vecs: bfloat16 [4, 2048, 1024], P('dp', 'ctx'), may hold values from -6 to 6
- value_vecs: bfloat16 [4, 2048, 1024], P('dp', 'ctx'), may hold values from -6 to 6
- out_grad: bfloat16 [4, 2048, 1024], P('dp', 'ctx'), may hold values from -6 to 6
- out_weight: bfloat16 [1024, 1024], P(('ctx', 'dp')), may hold values from -0.1875 to 0.1875
Outputs:
- query_grad: bfloat16 [4, 2048, 1024], P('dp', 'ctx')
- key_grad: bfloat16 [4, 2048, 1024], P('dp', 'ctx')
- value_grad: bfloat16 [4, 2048, 1024], P('dp', 'ctx')
- weight_grad: float32 [1024, 1024], P(('ctx', 'dp'))
The draws below stay inside these ranges and needn't reach their ends.
All inputs are finite; a program needn't handle non-finite values.
Results may differ from the reference program's by a relative error of at most 0.0057.
Values may be sent and summed in bfloat16 or wider, within the bound.
No kernel may reach another device: no remote copies, remote signals or barrier semaphores. Data moves between devices by JAX's collectives and lax.ppermute only.
A program may use at most 128 MiB of HBM per device.

```python
import math
import jax
import jax.numpy as jnp
from jax import lax

D = 1024
HEADS = 8
HEAD = 128
BLOCK = 256
TOK_DEV = 256
SEQLEN = 2048
SEQS = 4
N_CTX = 8
N_DP = 4


def levels(stream_key, dims, shards, low, largest):
    gain = 1.0
    for position, blocks in shards:
        draws = jax.random.uniform(jax.random.fold_in(jax.random.fold_in(stream_key, 6), position), (blocks,), jnp.float32, low / len(shards), largest / len(shards))
        gain = gain * jnp.repeat(jnp.exp(draws), dims[position] // blocks).reshape((-1,) + (1,) * (len(dims) - 1 - position))
    return gain


def scatter_about(key, dims, spread, bound, pieces=(), kind=jnp.bfloat16):
    result = spread * jax.random.normal(key, dims, jnp.float32)
    if pieces:
        result = result * levels(key, dims, pieces, -0.22, 0.18)
    return jnp.clip(result, -bound, bound).astype(kind)


def setup_inputs(seed: int = 0) -> dict:
    streams_of = jax.random.split(jax.random.key(seed), 6)
    queries = scatter_about(streams_of[0], (SEQS, SEQLEN, HEADS * HEAD), 1.0, 6.0, ((0, 4), (1, 8)))
    key_vecs = scatter_about(streams_of[1], (SEQS, SEQLEN, HEADS * HEAD), 1.0, 6.0, ((0, 4), (1, 8)))
    value_vecs = scatter_about(streams_of[2], (SEQS, SEQLEN, HEADS * HEAD), 1.0, 6.0, ((0, 4), (1, 8)))
    out_grad = scatter_about(streams_of[3], (SEQS, SEQLEN, D), 1.0, 6.0, ((0, 4), (1, 8)))
    out_weight = scatter_about(streams_of[4], (HEADS * HEAD, D), D ** -0.5, 0.1875, ((0, 32),))
    return dict(queries=queries, key_vecs=key_vecs, value_vecs=value_vecs, out_grad=out_grad, out_weight=out_weight)


def ein(form, left, right):
    return jnp.einsum(form, left.astype(jnp.float32), right.astype(jnp.float32))

def sequence_grads(qry_rows, key_rows, val_rows, grd_rows, att_scale):
    width = qry_rows.shape[-1]
    count = qry_rows.shape[0] // BLOCK

    def split(array):
        return array.reshape(count, BLOCK, HEADS, HEAD)
    qry_blk = split(qry_rows)
    key_blk = split(key_rows)
    val_blk = split(val_rows)
    grd_blk = split(grd_rows)
    kv_block = ein('bshe,bshf->bhef', key_blk, val_blk)
    qd_block = ein('bthf,bthe->bhfe', grd_blk, qry_blk)
    state_in = (jnp.cumsum(kv_block, 0) - kv_block).astype(jnp.bfloat16)
    carried = (jnp.cumsum(qd_block[::-1], 0)[::-1] - qd_block).astype(jnp.bfloat16)
    positions = jnp.arange(BLOCK)
    causal = positions[:, None] >= positions[None, :]
    scores = jnp.where(causal, ein('bthe,bshe->bhts', qry_blk, key_blk), 0.0).astype(jnp.bfloat16)
    attended = att_scale * (ein('bhts,bshf->bthf', scores, val_blk) + ein('bthe,bhef->bthf', qry_blk, state_in))
    dscores = jnp.where(causal, ein('bthf,bshf->bhts', grd_blk, val_blk), 0.0).astype(jnp.bfloat16)
    query_grad = att_scale * (ein('bhts,bshe->bthe', dscores, key_blk) + ein('bthf,bhef->bthe', grd_blk, state_in))
    key_grad = att_scale * (ein('bhts,bthe->bshe', dscores, qry_blk) + ein('bshf,bhfe->bshe', val_blk, carried))
    value_grad = att_scale * (ein('bhts,bthf->bshf', scores, grd_blk) + ein('bshe,bhfe->bshf', key_blk, carried))
    return (attended.astype(jnp.bfloat16).reshape(-1, width), query_grad.astype(jnp.bfloat16).reshape(-1, width), key_grad.astype(jnp.bfloat16).reshape(-1, width), value_grad.astype(jnp.bfloat16).reshape(-1, width))

def reference(queries, key_vecs, value_vecs, out_grad, out_weight):
    att_scale = 1.0 / math.sqrt(HEAD * TOK_DEV * N_CTX)
    inv_root = 1.0 / math.sqrt(N_DP * TOK_DEV * N_CTX)
    width = HEADS * HEAD
    flat_grad = out_grad.reshape(-1, D)
    att_grad = jnp.dot(flat_grad, out_weight.T, preferred_element_type=jnp.float32).astype(jnp.bfloat16)
    att_grad = att_grad.reshape(queries.shape[0], queries.shape[1], width)

    def one_sequence(members):
        return sequence_grads(members[0], members[1], members[2], members[3], att_scale)
    attended, query_grad, key_grad, value_grad = lax.map(one_sequence, (queries, key_vecs, value_vecs, att_grad))
    weight_grad = jnp.dot(attended.reshape(-1, width).T, flat_grad, preferred_element_type=jnp.float32) * inv_root
    return (query_grad, key_grad, value_grad, weight_grad)
```

```python
import functools
import math

import jax
import jax.numpy as jnp
from jax import lax
from jax.experimental import pallas as pl
from jax.experimental.pallas import tpu as pltpu
from jax.sharding import PartitionSpec as P

HEAD = 128
BLOCK = 256
BF = jnp.bfloat16
F32 = jnp.float32


def ein(form, left, right):
    return jnp.einsum(form, left, right, preferred_element_type=jnp.float32)


def nn(a, b):
    return lax.dot_general(a, b, (((1,), (0,)), ((), ())), preferred_element_type=F32)


def nt(a, b):
    return lax.dot_general(a, b, (((1,), (1,)), ((), ())), preferred_element_type=F32)


def tn(a, b):
    return lax.dot_general(a, b, (((0,), (0,)), ((), ())), preferred_element_type=F32)


def cols(index):
    return pl.ds(pl.multiple_of(index * HEAD, HEAD), HEAD)


def causal_mask():
    t = lax.broadcasted_iota(jnp.int32, (BLOCK, BLOCK), 0)
    s = lax.broadcasted_iota(jnp.int32, (BLOCK, BLOCK), 1)
    return t >= s


def place():
    me = lax.axis_index("ctx")
    return lax.rem(me, 2), lax.div(me, 2)


def local_call(kernel, outs, flops, *args):
    vmem = pl.BlockSpec(memory_space=pltpu.VMEM)
    size = sum(a.size * a.dtype.itemsize for a in args)
    size += sum(math.prod(s) * jnp.dtype(d).itemsize for s, d in outs)
    return pl.pallas_call(
        kernel,
        out_shape=[jax.ShapeDtypeStruct(s, d) for s, d in outs],
        in_specs=[vmem] * len(args),
        out_specs=[vmem] * len(outs),
        compiler_params=pltpu.CompilerParams(vmem_limit_bytes=24 << 20),
        cost_estimate=pl.CostEstimate(flops=flops, bytes_accessed=size, transcendentals=0),
    )(*args)


def kv_kernel(groups, k_o, v_o, k_r, v_r, kvsel, psum):
    par, _ = place()
    later = par.astype(F32)
    for j in range(groups):
        c = cols(2 * j + par)
        own = tn(k_o[:, c], v_o[:, c])
        other = tn(k_r[:, c], v_r[:, c])
        kvsel[j] = other * later + own * (1.0 - later)
        psum[j] = (own + other).astype(BF)


def intra_kernel(groups, q_o, k_o, v_o, q_r, k_r, v_r, intra):
    par, _ = place()
    mask = causal_mask()
    for i, (q, k, v) in enumerate(((q_o, k_o, v_o), (q_r, k_r, v_r))):
        for j in range(groups):
            c = cols(2 * j + par)
            scores = jnp.where(mask, nt(q[:, c], k[:, c]), 0.0).astype(BF)
            intra[i, :, j * HEAD : (j + 1) * HEAD] = nn(scores, v[:, c])


def attend_kernel(groups, att_scale, inv_root, q_o, q_r, g_o, g_r, intra, kvsel, *rest):
    parts = rest[: groups - 1]
    prod_own, prods, state_o, state_r = rest[groups - 1 :]
    par, chip = place()
    later = par.astype(F32)
    for m in range(groups - 1, -1, -1):
        j = lax.bitwise_xor(chip, m)
        total = sum(part[j].astype(F32) for part in parts)
        sel = kvsel[j]
        s_o = (total + later * sel).astype(BF)
        s_r = (total + (1.0 - later) * sel).astype(BF)
        state_o[j] = s_o
        state_r[j] = s_r
        c = cols(2 * j + par)
        a_o = (att_scale * (intra[0, :, cols(j)] + nn(q_o[:, c], s_o))).astype(BF)
        a_r = (att_scale * (intra[1, :, cols(j)] + nn(q_r[:, c], s_r))).astype(BF)
        term = (tn(a_o, g_o[...]) + tn(a_r, g_r[...])) * inv_root
        if m == 0:
            prod_own[...] = term
        else:
            prods[m - 1] = term.astype(BF)


def gather_kernel(n_dp, w_own, *rest):
    parts, full = rest[:-1], rest[-1]
    rows = w_own.shape[0]
    d = lax.axis_index("dp")
    for m, part in enumerate((w_own,) + tuple(parts)):
        at = pl.multiple_of(lax.bitwise_xor(d, m) * rows, rows)
        full[pl.ds(at, rows), :] = part[...]


def att_grad_kernel(groups, g_o, g_r, q_o, q_r, *rest):
    weights = rest[:groups]
    ag_o, ag_r, qdsel, psum = rest[groups:]
    par, chip = place()
    later = par.astype(F32)
    for m in range(groups):
        j = lax.bitwise_xor(chip, m)
        w = weights[m][...]
        a_o = nt(g_o[...], w).astype(BF)
        a_r = nt(g_r[...], w).astype(BF)
        ag_o[:, cols(j)] = a_o
        ag_r[:, cols(j)] = a_r
        c = cols(2 * j + par)
        own = tn(a_o, q_o[:, c])
        other = tn(a_r, q_r[:, c])
        qdsel[j] = own * later + other * (1.0 - later)
        psum[j] = (own + other).astype(BF)


def block_kernel(groups, att_scale, q_o, k_o, v_o, ag_o, ag_p, st_o, st_p, dq, dk_in, dv_in):
    par, _ = place()
    mask = causal_mask()
    for side, (ag, st) in enumerate(((ag_o, st_o), (ag_p, st_p))):
        parity = par if side == 0 else 1 - par
        for j in range(groups):
            c = cols(2 * j + parity)
            q, k, v, a = q_o[:, c], k_o[:, c], v_o[:, c], ag[:, j * HEAD : (j + 1) * HEAD]
            dscores = jnp.where(mask, nt(a, v), 0.0).astype(BF)
            scores = jnp.where(mask, nt(q, k), 0.0).astype(BF)
            dq[:, c] = (att_scale * (nn(dscores, k) + nt(a, st[j]))).astype(BF)
            dk_in[:, c] = tn(dscores, q)
            dv_in[:, c] = tn(scores, a)


def carried_kernel(groups, qdsel, *rest):
    parts = rest[: groups - 1]
    car_o, car_r = rest[groups - 1 :]
    par, _ = place()
    later = par.astype(F32)
    for j in range(groups):
        total = sum(part[j].astype(F32) for part in parts)
        sel = qdsel[j]
        car_o[j] = (total + (1.0 - later) * sel).astype(BF)
        car_r[j] = (total + later * sel).astype(BF)


def finish_kernel(groups, att_scale, k_o, v_o, car_o, car_p, dk_in, dv_in, dk, dv):
    par, _ = place()
    for side, car in enumerate((car_o, car_p)):
        parity = par if side == 0 else 1 - par
        for j in range(groups):
            c = cols(2 * j + parity)
            carried = car[j]
            dk[:, c] = (att_scale * (dk_in[:, c] + nn(v_o[:, c], carried))).astype(BF)
            dv[:, c] = (att_scale * (dv_in[:, c] + nt(k_o[:, c], carried))).astype(BF)


def fold_kernel(n_dp, prod_own, *rest):
    parts, (keep, send) = rest[:-2], rest[-2:]
    rows = keep.shape[0]
    d = lax.axis_index("dp")
    for m in range(n_dp):
        at = pl.ds(pl.multiple_of(lax.bitwise_xor(d, m) * rows, rows), rows)
        total = prod_own[at, :] + sum(part[at, :].astype(F32) for part in parts)
        if m == 0:
            keep[...] = total
        else:
            send[m - 1] = total.astype(BF)


def per_device(n_ctx, n_dp, queries, key_vecs, value_vecs, out_grad, out_weight):
    tok_count, width = queries.shape[1:]
    heads_n = width // HEAD
    groups = n_ctx // 2
    att_scale = 1.0 / math.sqrt(HEAD * tok_count * n_ctx)
    inv_root = 1.0 / math.sqrt(n_dp * tok_count * n_ctx)
    q_o, k_o, v_o, g_o = queries[0], key_vecs[0], value_vecs[0], out_grad[0]

    def core(x):
        return lax.ppermute(x, "ctx", [(i, i ^ 1) for i in range(n_ctx)])

    def chips(x, m):
        return lax.ppermute(x, "ctx", [(i, i ^ (2 * m)) for i in range(n_ctx)])

    def to_later(x, m):
        return lax.ppermute(x, "ctx", [(i, i ^ (2 * m)) for i in range(n_ctx) if i ^ (2 * m) > i])

    def to_earlier(x, m):
        return lax.ppermute(x, "ctx", [(i, i ^ (2 * m)) for i in range(n_ctx) if i ^ (2 * m) < i])

    def along_dp(x, m):
        return lax.ppermute(x, "dp", [(i, i ^ m) for i in range(n_dp)])

    others = range(1, groups)
    mat = HEAD * HEAD
    state_shape = (groups, HEAD, HEAD)
    half = groups * HEAD
    k_r, v_r = core(k_o), core(v_o)
    q_r, g_r = core(q_o), core(g_o)
    w_parts = [along_dp(out_weight, m) for m in range(1, n_dp)]
    kvsel, kv_sum = local_call(
        functools.partial(kv_kernel, groups),
        [(state_shape, F32), (state_shape, BF)],
        4 * groups * mat * BLOCK,
        k_o, v_o, k_r, v_r,
    )
    kv_parts = [to_later(kv_sum, m) for m in others]
    (w_head,) = local_call(
        functools.partial(gather_kernel, n_dp), [((HEAD, width), BF)], 0, out_weight, *w_parts
    )
    w_all = [w_head] + [chips(w_head, m) for m in others]
    (intra,) = local_call(
        functools.partial(intra_kernel, groups),
        [((2, BLOCK, half), F32)],
        8 * groups * BLOCK * BLOCK * HEAD,
        q_o, k_o, v_o, q_r, k_r, v_r,
    )
    prod_own, prods, state_o, state_r = local_call(
        functools.partial(attend_kernel, groups, att_scale, inv_root),
        [
            ((HEAD, width), F32),
            ((groups - 1, HEAD, width), BF),
            (state_shape, BF),
            (state_shape, BF),
        ],
        4 * groups * BLOCK * (mat + HEAD * width),
        q_o, q_r, g_o, g_r, intra, kvsel, *kv_parts,
    )
    terms = [chips(prods[m - 1], m) for m in others]
    state_p = core(state_r)
    ag_o, ag_r, qdsel, qd_sum = local_call(
        functools.partial(att_grad_kernel, groups),
        [((BLOCK, half), BF), ((BLOCK, half), BF), (state_shape, F32), (state_shape, BF)],
        4 * groups * BLOCK * (mat + HEAD * width),
        g_o, g_r, q_o, q_r, *w_all,
    )
    qd_parts = [to_earlier(qd_sum, m) for m in others]
    ag_p = core(ag_r)
    dq, dk_in, dv_in = local_call(
        functools.partial(block_kernel, groups, att_scale),
        [((BLOCK, width), BF), ((BLOCK, width), F32), ((BLOCK, width), F32)],
        4 * groups * BLOCK * HEAD * (5 * BLOCK + HEAD),
        q_o, k_o, v_o, ag_o, ag_p, state_o, state_p,
    )
    keep, send = local_call(
        functools.partial(fold_kernel, n_dp),
        [((HEAD // n_dp, width), F32), ((n_dp - 1, HEAD // n_dp, width), BF)],
        0,
        prod_own, *terms,
    )
    weight_grad = keep
    for m in range(1, n_dp):
        weight_grad = weight_grad + along_dp(send[m - 1], m).astype(F32)
    car_o, car_r = local_call(
        functools.partial(carried_kernel, groups),
        [(state_shape, BF), (state_shape, BF)],
        0,
        qdsel, *qd_parts,
    )
    car_p = core(car_r)
    dk, dv = local_call(
        functools.partial(finish_kernel, groups, att_scale),
        [((BLOCK, width), BF), ((BLOCK, width), BF)],
        8 * groups * BLOCK * mat,
        k_o, v_o, car_o, car_p, dk_in, dv_in,
    )
    return dq[None], dk[None], dv[None], weight_grad


def general_per_device(queries, key_vecs, value_vecs, out_grad, out_weight):
    qry_rows = queries[0]
    tok_count = qry_rows.shape[0]
    width = qry_rows.shape[1]
    heads_n = width // HEAD
    count = tok_count // BLOCK
    n_ctx = lax.axis_size("ctx")
    n_dp = lax.axis_size("dp")
    att_scale = 1.0 / math.sqrt(HEAD * tok_count * n_ctx)
    inv_root = 1.0 / math.sqrt(n_dp * tok_count * n_ctx)
    flat_grad = out_grad[0]

    def split(array):
        return array.reshape(count, BLOCK, heads_n, HEAD)

    qry_blk = split(qry_rows)
    key_blk = split(key_vecs[0])
    val_blk = split(value_vecs[0])
    kv_block = ein("bshe,bshf->bhef", key_blk, val_blk)
    local_kv = jnp.sum(kv_block, 0)
    grad_full = lax.dot_general(
        flat_grad,
        lax.all_gather(out_weight, ("ctx", "dp"), axis=0, tiled=True),
        (((1,), (1,)), ((), ())),
        preferred_element_type=jnp.float32,
    )
    att_grad = grad_full.astype(jnp.bfloat16)
    grd_blk = split(att_grad)
    qd_block = ein("bthf,bthe->bhfe", grd_blk, qry_blk)
    local_qd = jnp.sum(qd_block, 0)
    rows_each = heads_n * HEAD // n_ctx
    kv_parts, qd_parts = (
        lax.all_to_all(
            local_kv.reshape(n_ctx, rows_each, HEAD), "ctx", split_axis=0, concat_axis=0, tiled=True
        ),
        lax.all_to_all(
            local_qd.reshape(n_ctx, rows_each, HEAD), "ctx", split_axis=0, concat_axis=0, tiled=True
        ),
    )
    kv_earlier = jnp.cumsum(kv_parts, 0) - kv_parts
    qd_later = jnp.cumsum(qd_parts[::-1], 0)[::-1] - qd_parts
    kv_back, qd_back = (
        lax.all_to_all(kv_earlier, "ctx", split_axis=0, concat_axis=0, tiled=True),
        lax.all_to_all(qd_later, "ctx", split_axis=0, concat_axis=0, tiled=True),
    )
    kv_before = kv_back.reshape(local_kv.shape)
    qd_after = qd_back.reshape(local_qd.shape)
    state_in = (kv_before[None] + jnp.cumsum(kv_block, 0) - kv_block).astype(jnp.bfloat16)
    carried = (qd_after[None] + jnp.cumsum(qd_block[::-1], 0)[::-1] - qd_block).astype(jnp.bfloat16)
    positions = jnp.arange(BLOCK)
    causal = positions[:, None] >= positions[None, :]
    scores = jnp.where(causal, ein("bthe,bshe->bhts", qry_blk, key_blk), 0.0).astype(jnp.bfloat16)
    attended = att_scale * (
        ein("bhts,bshf->bthf", scores, val_blk) + ein("bthe,bhef->bthf", qry_blk, state_in)
    )
    attended = attended.astype(jnp.bfloat16).reshape(tok_count, width)
    weight_grad = lax.psum_scatter(
        lax.dot_general(
            attended, flat_grad, (((0,), (0,)), ((), ())), preferred_element_type=jnp.float32
        )
        * inv_root,
        ("ctx", "dp"),
        scatter_dimension=0,
        tiled=True,
    )
    dscores = jnp.where(causal, ein("bthf,bshf->bhts", grd_blk, val_blk), 0.0).astype(jnp.bfloat16)
    query_grad = att_scale * (
        ein("bhts,bshe->bthe", dscores, key_blk) + ein("bthf,bhef->bthe", grd_blk, state_in)
    )
    key_grad = att_scale * (
        ein("bhts,bthe->bshe", dscores, qry_blk) + ein("bshf,bhfe->bshe", val_blk, carried)
    )
    value_grad = att_scale * (
        ein("bhts,bthf->bshf", scores, grd_blk) + ein("bshe,bhfe->bshf", key_blk, carried)
    )
    shape_out = (1, tok_count, width)
    return (
        query_grad.astype(jnp.bfloat16).reshape(shape_out),
        key_grad.astype(jnp.bfloat16).reshape(shape_out),
        value_grad.astype(jnp.bfloat16).reshape(shape_out),
        weight_grad,
    )


def solution(mesh):
    placed = (
        P("dp", "ctx", None),
        P("dp", "ctx", None),
        P("dp", "ctx", None),
        P("dp", "ctx", None),
        P(("ctx", "dp"), None),
    )
    n_ctx, n_dp = mesh.shape["ctx"], mesh.shape["dp"]

    def chosen(queries, key_vecs, value_vecs, out_grad, out_weight):
        local = (queries, key_vecs, value_vecs, out_grad, out_weight)
        one_head = out_weight.shape[0] * n_dp == HEAD and HEAD % (16 * n_dp) == 0
        powers = n_ctx & (n_ctx - 1) == 0 and n_dp & (n_dp - 1) == 0 and n_ctx > 2
        if one_head and powers and queries.shape[:2] == (1, BLOCK):
            return per_device(n_ctx, n_dp, *local)
        return general_per_device(*local)

    return jax.shard_map(
        chosen,
        mesh=mesh,
        in_specs=placed,
        out_specs=(
            P("dp", "ctx", None),
            P("dp", "ctx", None),
            P("dp", "ctx", None),
            P(("ctx", "dp"), None),
        ),
        check_vma=False,
    )
```

```python
import functools
import math

import jax
import jax.numpy as jnp
from jax import lax
from jax.experimental import pallas as pl
from jax.experimental.pallas import tpu as pltpu
from jax.sharding import PartitionSpec as P

HEAD = 128
BLOCK = 256
GROUPS = 4
BF = jnp.bfloat16
F32 = jnp.float32


def ein(form, left, right):
    return jnp.einsum(form, left, right, preferred_element_type=jnp.float32)


def nn(a, b):
    return lax.dot_general(a, b, (((1,), (0,)), ((), ())), preferred_element_type=F32)


def nt(a, b):
    return lax.dot_general(a, b, (((1,), (1,)), ((), ())), preferred_element_type=F32)


def tn(a, b):
    return lax.dot_general(a, b, (((0,), (0,)), ((), ())), preferred_element_type=F32)


def cols(index):
    return pl.ds(pl.multiple_of(index * HEAD, HEAD), HEAD)


def causal_mask():
    t = lax.broadcasted_iota(jnp.int32, (BLOCK, BLOCK), 0)
    s = lax.broadcasted_iota(jnp.int32, (BLOCK, BLOCK), 1)
    return t >= s


def place():
    me = lax.axis_index("ctx")
    return lax.rem(me, 2), lax.div(me, 2)


def local_call(kernel, outs, *args, after=(), in_place=0, scratch=(), limit=24, micros=0):
    vmem = pl.BlockSpec(memory_space=pltpu.VMEM)
    hbm = pl.BlockSpec(memory_space=pltpu.HBM)
    anywhere = pl.BlockSpec(memory_space=pl.ANY)
    count = len(args)

    def body(*refs):
        kernel(*refs[:count], *refs[count + len(after) :])

    return pl.pallas_call(
        body,
        out_shape=[jax.ShapeDtypeStruct(s, d) for s, d in outs],
        in_specs=[vmem] * (count - in_place) + [hbm] * in_place + [anywhere] * len(after),
        out_specs=[vmem] * len(outs),
        scratch_shapes=scratch,
        compiler_params=pltpu.CompilerParams(vmem_limit_bytes=limit << 20),
        cost_estimate=pl.CostEstimate(
            flops=0, bytes_accessed=micros * 3_600_000, transcendentals=0
        ),
    )(*args, *after)


def kv_kernel(kv_o, kv_r, w_o, w_again, kvsel, psum, psum_sent):
    par, _ = place()
    later = par.astype(F32)
    for j in range(GROUPS):
        c = cols(2 * j + par)
        own = tn(kv_o[0, :, c], kv_o[1, :, c])
        other = tn(kv_r[0, :, c], kv_r[1, :, c])
        kvsel[j] = other * later + own * (1.0 - later)
        psum[j] = own + other
        psum_sent[j] = (own + other).astype(BF)
    w_again[...] = w_o[...]


def total_kernel(psum, received, total):
    total[...] = (psum[...] + received[...].astype(F32)).astype(BF)


def intra_kernel(qg_o, kv_o, qg_r, kv_r, intra):
    par, _ = place()
    mask = causal_mask()
    for i, (qg, kv) in enumerate(((qg_o, kv_o), (qg_r, kv_r))):
        for j in range(GROUPS):
            c = cols(2 * j + par)
            scores = jnp.where(mask, nt(qg[0, :, c], kv[0, :, c]), 0.0).astype(BF)
            intra[i, :, j * HEAD : (j + 1) * HEAD] = nn(scores, kv[1, :, c])


def attend_kernel(
    att_scale, inv_root, qg_o, qg_r, intra, kvsel, kv_x, kv_y,
    to_x, to_y, keep, forward, state_o, state_r,
):
    par, chip = place()
    later = par.astype(F32)
    x_later = lax.rem(chip, 2).astype(F32)
    half = qg_o.shape[2] // 2
    for m in (3, 1, 2, 0):
        j = lax.bitwise_xor(chip, m)
        earlier = kv_x[j].astype(F32) * x_later + kv_y[j].astype(F32)
        sel = kvsel[j]
        s_o = (earlier + later * sel).astype(BF)
        s_r = (earlier + (1.0 - later) * sel).astype(BF)
        state_o[j] = s_o
        state_r[j] = s_r
        c = cols(2 * j + par)
        a_o = (att_scale * (intra[0, :, cols(j)] + nn(qg_o[0, :, c], s_o))).astype(BF)
        a_r = (att_scale * (intra[1, :, cols(j)] + nn(qg_r[0, :, c], s_r))).astype(BF)
        term = (tn(a_o, qg_o[1]) + tn(a_r, qg_r[1])) * inv_root
        first, second = term[:, :half], term[:, half:]
        if m == 3:
            to_x[1], to_y[1] = first.astype(BF), second.astype(BF)
        elif m == 1:
            to_x[0], forward[1] = first.astype(BF), second
        elif m == 2:
            forward[0], to_y[0] = first, second.astype(BF)
        else:
            keep[...] = term


def forward_kernel(side, forward, received, total):
    total[...] = (forward[side] + received[1].astype(F32)).astype(BF)


def fold_kernel(n_dp, keep, from_x, from_y, last_y, last_x, own, *send):
    rows = own.shape[0]
    half = keep.shape[1] // 2
    d = lax.axis_index("dp")
    for m in range(n_dp):
        at = pl.ds(pl.multiple_of(lax.bitwise_xor(d, m) * rows, rows), rows)
        for side, (one, two) in enumerate(((from_x, last_y), (from_y, last_x))):
            c = slice(side * half, (side + 1) * half)
            total = keep[at, c] + one[0, at, :].astype(F32) + two[at, :].astype(F32)
            if m == 0:
                own[:, c] = total
            else:
                send[m - 1][:, c] = total.astype(BF)


def sum_kernel(own, *rest):
    parts, (total, done) = rest[:-2], rest[-2:]
    done[...] = jnp.zeros_like(done)
    total[...] = own[...] + sum(part[...].astype(F32) for part in parts)


def order_kernel(n_dp, first, *refs):
    parts, full = refs[:-1], refs[-1]
    rows = full.shape[0] // n_dp
    d = lax.axis_index("dp")
    if first:
        full[...] = parts[0][...]
        parts = parts[1:]
    for m, part in enumerate(parts, first):
        at = pl.multiple_of(lax.bitwise_xor(d, m) * rows, rows)
        full[pl.ds(at, rows), :] = part[...]


def att_grad_kernel(qg_o, qg_r, w_0, w_x, w_y, w_d0, w_d1, ag_o, ag_r, qdsel, psum, psum_sent):
    par, chip = place()
    later = par.astype(F32)
    for m, weight in enumerate((w_0, w_x, w_y, None)):
        j = lax.bitwise_xor(chip, m)
        if weight is None:
            a_o, a_r = (
                jnp.concatenate([nt(g[1], w_d0[...]), nt(g[1], w_d1[...])], axis=1).astype(BF)
                for g in (qg_o, qg_r)
            )
        else:
            a_o, a_r = (nt(g[1], weight[...]).astype(BF) for g in (qg_o, qg_r))
        ag_o[:, cols(j)] = a_o
        ag_r[:, cols(j)] = a_r
        c = cols(2 * j + par)
        own = tn(a_o, qg_o[0, :, c])
        other = tn(a_r, qg_r[0, :, c])
        qdsel[j] = own * later + other * (1.0 - later)
        psum[j] = own + other
        psum_sent[j] = (own + other).astype(BF)


def block_kernel(att_scale, qg_o, kv_o, ag_o, ag_p, st_o, st_p, dq, dk_in, dv_in):
    par, _ = place()
    mask = causal_mask()
    for side, (ag, st) in enumerate(((ag_o, st_o), (ag_p, st_p))):
        parity = par if side == 0 else 1 - par
        for j in range(GROUPS):
            c = cols(2 * j + parity)
            q, k, v = qg_o[0, :, c], kv_o[0, :, c], kv_o[1, :, c]
            a = ag[:, j * HEAD : (j + 1) * HEAD]
            dscores = jnp.where(mask, nt(a, v), 0.0).astype(BF)
            scores = jnp.where(mask, nt(q, k), 0.0).astype(BF)
            dq[:, c] = (att_scale * (nn(dscores, k) + nt(a, st[j]))).astype(BF)
            dk_in[:, c] = tn(dscores, q)
            dv_in[:, c] = tn(scores, a)


def carried_kernel(qdsel, qd_x, qd_y, car_o, car_r):
    par, chip = place()
    later = par.astype(F32)
    x_earlier = (1 - lax.rem(chip, 2)).astype(F32)
    for j in range(GROUPS):
        total = qd_x[j].astype(F32) * x_earlier + qd_y[j].astype(F32)
        sel = qdsel[j]
        car_o[j] = (total + (1.0 - later) * sel).astype(BF)
        car_r[j] = (total + later * sel).astype(BF)


def finish_kernel(att_scale, kv_o, car_o, car_p, dk_in, dv_in, dk, dv):
    par, _ = place()
    for side, car in enumerate((car_o, car_p)):
        parity = par if side == 0 else 1 - par
        for j in range(GROUPS):
            c = cols(2 * j + parity)
            carried = car[j]
            dk[:, c] = (att_scale * (dk_in[:, c] + nn(kv_o[1, :, c], carried))).astype(BF)
            dv[:, c] = (att_scale * (dv_in[:, c] + nt(kv_o[0, :, c], carried))).astype(BF)


def per_device(n_ctx, n_dp, queries, key_vecs, value_vecs, out_grad, out_weight):
    tok_count, width = queries.shape[1:]
    att_scale = 1.0 / math.sqrt(HEAD * tok_count * n_ctx)
    inv_root = 1.0 / math.sqrt(n_dp * tok_count * n_ctx)

    def along(bit, keep=lambda i: True):
        return [(i, i ^ bit) for i in range(n_ctx) if keep(i)]

    def core(x):
        return lax.ppermute(x, "ctx", along(1))

    def over_x(x):
        return lax.ppermute(x, "ctx", along(2))

    def over_y(x):
        return lax.ppermute(x, "ctx", along(4))

    def along_dp(x, m):
        return lax.ppermute(x, "dp", [(i, i ^ m) for i in range(n_dp)])

    state = (GROUPS, HEAD, HEAD)
    half = width // 2
    rows = HEAD // n_dp
    kv_o = jnp.concatenate([key_vecs, value_vecs])
    qg_o = jnp.concatenate([queries, out_grad])
    kv_r = core(kv_o)
    w_parts = [along_dp(out_weight, 1)]
    w_again, kvsel, kv_own, kv_sent = local_call(
        kv_kernel,
        [((rows, width), BF), (state, F32), (state, F32), (state, BF)],
        kv_o, kv_r, out_weight,
    )
    kv_x = over_x(kv_sent)
    w_parts += [along_dp(w_again, m) for m in range(2, n_dp)]
    qg_r = core(qg_o)
    (w_two,) = local_call(
        functools.partial(order_kernel, n_dp, 0), [((HEAD, width), BF)], w_again, w_parts[0],
        micros=10,
    )
    (intra,) = local_call(
        intra_kernel, [((2, BLOCK, half), F32)], qg_o, kv_o, qg_r, kv_r, after=(w_two,)
    )
    (kv_total,) = local_call(total_kernel, [(state, BF)], kv_own, kv_x, after=(intra,))
    kv_y = lax.ppermute(kv_total, "ctx", along(4, lambda i: i < i ^ 4))
    (w_0,) = local_call(
        functools.partial(order_kernel, n_dp, 2),
        [((HEAD, width), BF)], w_two, *w_parts[1:], after=(kv_total,),
    )
    w_x, w_y = over_x(w_0), over_y(w_0)
    w_d0, w_d1 = over_y(w_x[: HEAD // 2]), over_x(w_y[HEAD // 2 :])
    to_x, to_y, keep, forward, state_o, state_r = local_call(
        functools.partial(attend_kernel, att_scale, inv_root),
        [
            ((2, HEAD, half), BF),
            ((2, HEAD, half), BF),
            ((HEAD, width), F32),
            ((2, HEAD, half), F32),
            (state, BF),
            (state, BF),
        ],
        qg_o, qg_r, intra, kvsel, kv_x, kv_y,
        after=(w_0,),
    )
    from_x, from_y = over_x(to_x), over_y(to_y)
    state_p = core(state_r)
    (pass_y,) = local_call(
        functools.partial(forward_kernel, 0), [((HEAD, half), BF)], forward, from_x
    )
    (pass_x,) = local_call(
        functools.partial(forward_kernel, 1), [((HEAD, half), BF)], forward, from_y,
        after=(pass_y,),
    )
    last_y, last_x = over_y(pass_y), over_x(pass_x)
    ag_o, ag_r, qdsel, qd_own, qd_sent = local_call(
        att_grad_kernel,
        [((BLOCK, half), BF), ((BLOCK, half), BF), (state, F32), (state, F32), (state, BF)],
        qg_o, qg_r, w_0, w_x, w_y, w_d0, w_d1,
        after=(pass_y, pass_x),
    )
    qd_x = over_x(qd_sent)
    ag_p = core(ag_r)
    own, *send = local_call(
        functools.partial(fold_kernel, n_dp),
        [((rows, width), F32)] + [((rows, width), BF)] * (n_dp - 1),
        keep, from_x, from_y, last_y, last_x,
        after=(qd_sent,),
    )
    got = [along_dp(send[m - 1], m) for m in range(1, n_dp)]
    (qd_total,) = local_call(total_kernel, [(state, BF)], qd_own, qd_x, after=(send[0],))
    qd_y = lax.ppermute(qd_total, "ctx", along(4, lambda i: i > i ^ 4))
    dq, dk_in, dv_in = local_call(
        functools.partial(block_kernel, att_scale),
        [((BLOCK, width), BF), ((BLOCK, width), F32), ((BLOCK, width), F32)],
        qg_o, kv_o, ag_o, ag_p, state_o, state_p,
        after=(qd_total,),
    )
    weight_grad, summed = local_call(
        sum_kernel, [((rows, width), F32), ((8, HEAD), F32)], own, *got, after=(dk_in,)
    )
    car_o, car_r = local_call(
        carried_kernel, [(state, BF), (state, BF)], qdsel, qd_x, qd_y, after=(summed,)
    )
    car_p = core(car_r)
    dk, dv = local_call(
        functools.partial(finish_kernel, att_scale),
        [((BLOCK, width), BF), ((BLOCK, width), BF)],
        kv_o, car_o, car_p, dk_in, dv_in,
    )
    return dq[None], dk[None], dv[None], weight_grad


def general_per_device(queries, key_vecs, value_vecs, out_grad, out_weight):
    qry_rows = queries[0]
    tok_count = qry_rows.shape[0]
    width = qry_rows.shape[1]
    heads_n = width // HEAD
    count = tok_count // BLOCK
    n_ctx = lax.axis_size("ctx")
    n_dp = lax.axis_size("dp")
    att_scale = 1.0 / math.sqrt(HEAD * tok_count * n_ctx)
    inv_root = 1.0 / math.sqrt(n_dp * tok_count * n_ctx)
    flat_grad = out_grad[0]

    def split(array):
        return array.reshape(count, BLOCK, heads_n, HEAD)

    qry_blk = split(qry_rows)
    key_blk = split(key_vecs[0])
    val_blk = split(value_vecs[0])
    kv_block = ein("bshe,bshf->bhef", key_blk, val_blk)
    local_kv = jnp.sum(kv_block, 0)
    grad_full = lax.dot_general(
        flat_grad,
        lax.all_gather(out_weight, ("ctx", "dp"), axis=0, tiled=True),
        (((1,), (1,)), ((), ())),
        preferred_element_type=jnp.float32,
    )
    att_grad = grad_full.astype(jnp.bfloat16)
    grd_blk = split(att_grad)
    qd_block = ein("bthf,bthe->bhfe", grd_blk, qry_blk)
    local_qd = jnp.sum(qd_block, 0)
    rows_each = heads_n * HEAD // n_ctx
    kv_parts, qd_parts = (
        lax.all_to_all(
            local_kv.reshape(n_ctx, rows_each, HEAD), "ctx", split_axis=0, concat_axis=0, tiled=True
        ),
        lax.all_to_all(
            local_qd.reshape(n_ctx, rows_each, HEAD), "ctx", split_axis=0, concat_axis=0, tiled=True
        ),
    )
    kv_earlier = jnp.cumsum(kv_parts, 0) - kv_parts
    qd_later = jnp.cumsum(qd_parts[::-1], 0)[::-1] - qd_parts
    kv_back, qd_back = (
        lax.all_to_all(kv_earlier, "ctx", split_axis=0, concat_axis=0, tiled=True),
        lax.all_to_all(qd_later, "ctx", split_axis=0, concat_axis=0, tiled=True),
    )
    kv_before = kv_back.reshape(local_kv.shape)
    qd_after = qd_back.reshape(local_qd.shape)
    state_in = (kv_before[None] + jnp.cumsum(kv_block, 0) - kv_block).astype(jnp.bfloat16)
    carried = (qd_after[None] + jnp.cumsum(qd_block[::-1], 0)[::-1] - qd_block).astype(jnp.bfloat16)
    positions = jnp.arange(BLOCK)
    causal = positions[:, None] >= positions[None, :]
    scores = jnp.where(causal, ein("bthe,bshe->bhts", qry_blk, key_blk), 0.0).astype(jnp.bfloat16)
    attended = att_scale * (
        ein("bhts,bshf->bthf", scores, val_blk) + ein("bthe,bhef->bthf", qry_blk, state_in)
    )
    attended = attended.astype(jnp.bfloat16).reshape(tok_count, width)
    weight_grad = lax.psum_scatter(
        lax.dot_general(
            attended, flat_grad, (((0,), (0,)), ((), ())), preferred_element_type=jnp.float32
        )
        * inv_root,
        ("ctx", "dp"),
        scatter_dimension=0,
        tiled=True,
    )
    dscores = jnp.where(causal, ein("bthf,bshf->bhts", grd_blk, val_blk), 0.0).astype(jnp.bfloat16)
    query_grad = att_scale * (
        ein("bhts,bshe->bthe", dscores, key_blk) + ein("bthf,bhef->bthe", grd_blk, state_in)
    )
    key_grad = att_scale * (
        ein("bhts,bthe->bshe", dscores, qry_blk) + ein("bshf,bhfe->bshe", val_blk, carried)
    )
    value_grad = att_scale * (
        ein("bhts,bthf->bshf", scores, grd_blk) + ein("bshe,bhfe->bshf", key_blk, carried)
    )
    shape_out = (1, tok_count, width)
    return (
        query_grad.astype(jnp.bfloat16).reshape(shape_out),
        key_grad.astype(jnp.bfloat16).reshape(shape_out),
        value_grad.astype(jnp.bfloat16).reshape(shape_out),
        weight_grad,
    )


def solution(mesh):
    placed = (
        P("dp", "ctx", None),
        P("dp", "ctx", None),
        P("dp", "ctx", None),
        P("dp", "ctx", None),
        P(("ctx", "dp"), None),
    )
    n_ctx, n_dp = mesh.shape["ctx"], mesh.shape["dp"]

    def chosen(queries, key_vecs, value_vecs, out_grad, out_weight):
        local = (queries, key_vecs, value_vecs, out_grad, out_weight)
        one_head = out_weight.shape[0] * n_dp == HEAD and n_ctx == 2 * GROUPS
        if one_head and n_dp in (2, 4, 8) and queries.shape[:2] == (1, BLOCK):
            return per_device(n_ctx, n_dp, *local)
        return general_per_device(*local)

    return jax.shard_map(
        chosen,
        mesh=mesh,
        in_specs=placed,
        out_specs=(
            P("dp", "ctx", None),
            P("dp", "ctx", None),
            P("dp", "ctx", None),
            P(("ctx", "dp"), None),
        ),
        check_vma=False,
    )
```

```python
import functools
import math

import jax
import jax.numpy as jnp
from jax import lax
from jax.experimental import pallas as pl
from jax.experimental.pallas import tpu as pltpu
from jax.sharding import PartitionSpec as P

HEAD = 128
BLOCK = 256
GROUPS = 4
BF = jnp.bfloat16
F32 = jnp.float32


def ein(form, left, right):
    return jnp.einsum(form, left, right, preferred_element_type=jnp.float32)


def nn(a, b):
    return lax.dot_general(a, b, (((1,), (0,)), ((), ())), preferred_element_type=F32)


def nt(a, b):
    return lax.dot_general(a, b, (((1,), (1,)), ((), ())), preferred_element_type=F32)


def tn(a, b):
    return lax.dot_general(a, b, (((0,), (0,)), ((), ())), preferred_element_type=F32)


def cols(index):
    return pl.ds(pl.multiple_of(index * HEAD, HEAD), HEAD)


def causal_mask():
    t = lax.broadcasted_iota(jnp.int32, (BLOCK, BLOCK), 0)
    s = lax.broadcasted_iota(jnp.int32, (BLOCK, BLOCK), 1)
    return t >= s


def place():
    me = lax.axis_index("ctx")
    return lax.rem(me, 2), lax.div(me, 2)


def local_call(kernel, outs, *args, after=(), scratch=(), streamed=False, micros=0.0):
    vmem = pl.BlockSpec(memory_space=pltpu.VMEM)
    anywhere = pl.BlockSpec(memory_space=pl.ANY)
    count = len(args)

    def body(*refs):
        kernel(*refs[:count], *refs[count + len(after) :])

    return pl.pallas_call(
        body,
        out_shape=[jax.ShapeDtypeStruct(s, d) for s, d in outs],
        in_specs=[vmem] * count + [anywhere] * len(after),
        out_specs=[anywhere if streamed else vmem] * len(outs),
        scratch_shapes=scratch,
        compiler_params=pltpu.CompilerParams(vmem_limit_bytes=24 << 20),
        cost_estimate=pl.CostEstimate(
            flops=int(micros * 1e9), bytes_accessed=int(micros * 3.6e6), transcendentals=0
        ),
    )(*args, *after)


def kv_kernel(kv_o, k_r, v_r, kvsel, psum_sent):
    par, _ = place()
    later = par.astype(F32)
    for j in range(GROUPS):
        c = cols(2 * j + par)
        own = tn(kv_o[0, :, c], kv_o[1, :, c])
        other = tn(k_r[:, c], v_r[:, c])
        kvsel[j] = other * later + own * (1.0 - later)
        psum_sent[j] = (own + other).astype(BF)


def pack_kernel(first, second, both):
    both[0], both[1] = first[...], second[...]


def intra_kernel(qg_o, kv_o, qg_r, k_r, v_r, intra):
    par, _ = place()
    mask = causal_mask()
    kv_both = ((kv_o.at[0], kv_o.at[1]), (k_r, v_r))
    for i, (qg, (k, v)) in enumerate(zip((qg_o, qg_r), kv_both)):
        for j in range(GROUPS):
            c = cols(2 * j + par)
            scores = jnp.where(mask, nt(qg[0, :, c], k[:, c]), 0.0).astype(BF)
            intra[i, :, j * HEAD : (j + 1) * HEAD] = nn(scores, v[:, c])


def attend_kernel(
    att_scale, inv_root, qg_o, qg_r, intra, kvsel, kv_x, kv_y, kv_d,
    to_x, to_y, keep, forward, state_o, state_r,
):
    par, chip = place()
    later = par.astype(F32)
    x_later = lax.rem(chip, 2).astype(F32)
    y_later = lax.div(chip, 2).astype(F32)
    half = qg_o.shape[2] // 2
    for m in (3, 1, 2, 0):
        j = lax.bitwise_xor(chip, m)
        earlier = kv_x[j].astype(F32) * x_later
        earlier += (kv_y[j].astype(F32) + kv_d[j].astype(F32)) * y_later
        sel = kvsel[j]
        s_o = (earlier + later * sel).astype(BF)
        s_r = (earlier + (1.0 - later) * sel).astype(BF)
        state_o[j] = s_o
        state_r[j] = s_r
        c = cols(2 * j + par)
        a_o = (att_scale * (intra[0, :, cols(j)] + nn(qg_o[0, :, c], s_o))).astype(BF)
        a_r = (att_scale * (intra[1, :, cols(j)] + nn(qg_r[0, :, c], s_r))).astype(BF)
        term = (tn(a_o, qg_o[1]) + tn(a_r, qg_r[1])) * inv_root
        first, second = term[:, :half], term[:, half:]
        if m == 3:
            to_x[1], to_y[1] = first.astype(BF), second.astype(BF)
        elif m == 1:
            to_x[0], forward[1] = first.astype(BF), second
        elif m == 2:
            forward[0], to_y[0] = first, second.astype(BF)
        else:
            keep[...] = term


def forward_kernel(side, forward, received, total):
    total[...] = (forward[side] + received[1].astype(F32)).astype(BF)


def fold_kernel(n_dp, keep, from_x, from_y, last_y, last_x, own, *send):
    rows = own.shape[0]
    half = keep.shape[1] // 2
    d = lax.axis_index("dp")
    for m in range(n_dp):
        at = pl.ds(pl.multiple_of(lax.bitwise_xor(d, m) * rows, rows), rows)
        for side, (one, two) in enumerate(((from_x, last_y), (from_y, last_x))):
            c = slice(side * half, (side + 1) * half)
            total = keep[at, c] + one[0, at, :].astype(F32) + two[at, :].astype(F32)
            if m == 0:
                own[:, c] = total
            else:
                send[m - 1][:, c] = total.astype(BF)


def sum_kernel(own, *rest):
    parts, total = rest[:-1], rest[-1]
    total[...] = own[...] + sum(part[...].astype(F32) for part in parts)


def order_kernel(n_dp, *refs):
    parts, full = refs[:-1], refs[-1]
    rows = parts[0].shape[0]
    d = lax.axis_index("dp")
    for m, part in enumerate(parts):
        at = pl.multiple_of(lax.bitwise_xor(d, m) * rows, rows)
        full[pl.ds(at, rows), :] = part[...]


def head_grad(m, weights, qg_o, qg_r, ag_o, ag_r, qdsel, psum_sent):
    par, chip = place()
    later = par.astype(F32)
    j = lax.bitwise_xor(chip, m)
    c = cols(2 * j + par)
    a_o, a_r = (
        jnp.concatenate([nt(qg[1], w[...]) for w in weights], axis=1).astype(BF)
        for qg in (qg_o, qg_r)
    )
    ag_o[:, cols(j)] = a_o
    ag_r[:, cols(j)] = a_r
    own = tn(a_o, qg_o[0, :, c])
    other = tn(a_r, qg_r[0, :, c])
    qdsel[j] = own * later + other * (1.0 - later)
    psum_sent[j] = (own + other).astype(BF)


def near_grad_kernel(qg_o, qg_r, w_0, w_x, w_y, *outs):
    for m, weight in enumerate((w_0, w_x, w_y)):
        head_grad(m, (weight,), qg_o, qg_r, *outs)


def far_grad_kernel(qg_o, qg_r, w_d0, w_d1, *rest):
    near, outs = rest[: len(rest) // 2], rest[len(rest) // 2 :]
    for src, dst in zip(near, outs):
        dst[...] = src[...]
    head_grad(3, (w_d0, w_d1), qg_o, qg_r, *outs)


def block_kernel(att_scale, qg_o, kv_o, ag_o, ag_p, st_o, st_p, dq, dk_in, dv_in):
    par, _ = place()
    mask = causal_mask()
    for side, (ag, st) in enumerate(((ag_o, st_o), (ag_p, st_p))):
        parity = par if side == 0 else 1 - par
        for j in range(GROUPS):
            c = cols(2 * j + parity)
            q, k, v = qg_o[0, :, c], kv_o[0, :, c], kv_o[1, :, c]
            a = ag[:, j * HEAD : (j + 1) * HEAD]
            dscores = jnp.where(mask, nt(a, v), 0.0).astype(BF)
            scores = jnp.where(mask, nt(q, k), 0.0).astype(BF)
            dq[:, c] = (att_scale * (nn(dscores, k) + nt(a, st[j]))).astype(BF)
            dk_in[:, c] = tn(dscores, q)
            dv_in[:, c] = tn(scores, a)


def carried_kernel(qdsel, qd_x, qd_y, qd_d, car_o, car_r):
    par, chip = place()
    later = par.astype(F32)
    x_earlier = (1 - lax.rem(chip, 2)).astype(F32)
    y_earlier = (1 - lax.div(chip, 2)).astype(F32)
    for j in range(GROUPS):
        total = qd_x[j].astype(F32) * x_earlier
        total += (qd_y[j].astype(F32) + qd_d[j].astype(F32)) * y_earlier
        sel = qdsel[j]
        car_o[j] = (total + (1.0 - later) * sel).astype(BF)
        car_r[j] = (total + later * sel).astype(BF)


def finish_kernel(
    att_scale, kv_o, car_o, car_p, dk_in, dv_in, summed, dk, dv, weight_grad, dk_here, dv_here, sems
):
    par, _ = place()
    copies = [pltpu.make_async_copy(summed, weight_grad, sems.at[4 * GROUPS])]
    copies[0].start()
    for side, car in enumerate((car_o, car_p)):
        parity = par if side == 0 else 1 - par
        for j in range(GROUPS):
            c = cols(2 * j + parity)
            carried = car[j]
            dk_here[:, c] = (att_scale * (dk_in[:, c] + nn(kv_o[1, :, c], carried))).astype(BF)
            dv_here[:, c] = (att_scale * (dv_in[:, c] + nt(kv_o[0, :, c], carried))).astype(BF)
            for here, out in ((dk_here, dk), (dv_here, dv)):
                sem = sems.at[len(copies) - 1]
                copies.append(pltpu.make_async_copy(here.at[:, c], out.at[:, c], sem))
                copies[-1].start()
    for copy in copies:
        copy.wait()


def per_device(n_ctx, n_dp, queries, key_vecs, value_vecs, out_grad, out_weight):
    tok_count, width = queries.shape[1:]
    att_scale = 1.0 / math.sqrt(HEAD * tok_count * n_ctx)
    inv_root = 1.0 / math.sqrt(n_dp * tok_count * n_ctx)

    def along(bit):
        return [(i, i ^ bit) for i in range(n_ctx)]

    def core(x):
        return lax.ppermute(x, "ctx", along(1))

    def over_x(x):
        return lax.ppermute(x, "ctx", along(2))

    def over_y(x):
        return lax.ppermute(x, "ctx", along(4))

    def over_both(x):
        return lax.ppermute(x, "ctx", along(6))

    def along_dp(x, m):
        return lax.ppermute(x, "dp", [(i, i ^ m) for i in range(n_dp)])

    state = (GROUPS, HEAD, HEAD)
    half = width // 2
    rows = HEAD // n_dp
    k_r, v_r = core(key_vecs[0]), core(value_vecs[0])
    kv_o = jnp.concatenate([key_vecs, value_vecs])
    w_parts = [along_dp(out_weight, m) for m in range(1, n_dp)]
    kvsel, kv_sent = local_call(
        kv_kernel,
        [(state, F32), (state, BF)],
        kv_o, k_r, v_r,
    )
    (qg_o,) = local_call(
        pack_kernel, [((2, BLOCK, width), BF)], queries[0], out_grad[0], after=(kv_sent,)
    )
    kv_x, kv_y, kv_d = over_x(kv_sent), over_y(kv_sent), over_both(kv_sent)
    qg_r = core(qg_o)
    (w_0,) = local_call(
        functools.partial(order_kernel, n_dp),
        [((HEAD, width), BF)], out_weight, *w_parts, after=(qg_o,), micros=20,
    )
    (intra,) = local_call(
        intra_kernel,
        [((2, BLOCK, half), F32)], qg_o, kv_o, qg_r, k_r, v_r, after=(w_0,),
    )
    w_x, w_y = over_x(w_0), over_y(w_0)
    w_d0, w_d1 = over_y(w_x[: HEAD // 2]), over_x(w_y[HEAD // 2 :])
    to_x, to_y, keep, forward, state_o, state_r = local_call(
        functools.partial(attend_kernel, att_scale, inv_root),
        [
            ((2, HEAD, half), BF),
            ((2, HEAD, half), BF),
            ((HEAD, width), F32),
            ((2, HEAD, half), F32),
            (state, BF),
            (state, BF),
        ],
        qg_o, qg_r, intra, kvsel, kv_x, kv_y, kv_d,
    )
    from_x, from_y = over_x(to_x), over_y(to_y)
    state_p = core(state_r)
    grads = [((BLOCK, half), BF), ((BLOCK, half), BF), (state, F32), (state, BF)]
    near = local_call(near_grad_kernel, grads, qg_o, qg_r, w_0, w_x, w_y, after=(to_x,))
    (pass_y,) = local_call(
        functools.partial(forward_kernel, 0), [((HEAD, half), BF)], forward, from_x,
        after=(near[3],),
    )
    (pass_x,) = local_call(
        functools.partial(forward_kernel, 1), [((HEAD, half), BF)], forward, from_y,
        after=(pass_y,),
    )
    last_y, last_x = over_y(pass_y), over_x(pass_x)
    ag_o, ag_r, qdsel, qd_sent = local_call(
        far_grad_kernel, grads, qg_o, qg_r, w_d0, w_d1, *near, after=(pass_x,)
    )
    qd_x, qd_y, qd_d = over_x(qd_sent), over_y(qd_sent), over_both(qd_sent)
    ag_p = core(ag_r)
    own, *send = local_call(
        functools.partial(fold_kernel, n_dp),
        [((rows, width), F32)] + [((rows, width), BF)] * (n_dp - 1),
        keep, from_x, from_y, last_y, last_x,
        after=(qd_sent,), micros=20,
    )
    got = [along_dp(send[m - 1], m) for m in range(1, n_dp)]
    dq, dk_in, dv_in = local_call(
        functools.partial(block_kernel, att_scale),
        [((BLOCK, width), BF), ((BLOCK, width), F32), ((BLOCK, width), F32)],
        qg_o, kv_o, ag_o, ag_p, state_o, state_p,
        after=(send[0],),
    )
    car_o, car_r = local_call(
        carried_kernel, [(state, BF), (state, BF)], qdsel, qd_x, qd_y, qd_d, after=(dk_in,)
    )
    car_p = core(car_r)
    (summed,) = local_call(
        sum_kernel, [((rows, width), F32)], own, *got, after=(car_r,), micros=20
    )
    dk, dv, weight_grad = local_call(
        functools.partial(finish_kernel, att_scale),
        [((BLOCK, width), BF), ((BLOCK, width), BF), ((rows, width), F32)],
        kv_o, car_o, car_p, dk_in, dv_in, summed,
        streamed=True,
        scratch=[
            pltpu.VMEM((BLOCK, width), BF),
            pltpu.VMEM((BLOCK, width), BF),
            pltpu.SemaphoreType.DMA((4 * GROUPS + 1,)),
        ],
    )
    return dq[None], dk[None], dv[None], weight_grad


def general_per_device(queries, key_vecs, value_vecs, out_grad, out_weight):
    qry_rows = queries[0]
    tok_count = qry_rows.shape[0]
    width = qry_rows.shape[1]
    heads_n = width // HEAD
    count = tok_count // BLOCK
    n_ctx = lax.axis_size("ctx")
    n_dp = lax.axis_size("dp")
    att_scale = 1.0 / math.sqrt(HEAD * tok_count * n_ctx)
    inv_root = 1.0 / math.sqrt(n_dp * tok_count * n_ctx)
    flat_grad = out_grad[0]

    def split(array):
        return array.reshape(count, BLOCK, heads_n, HEAD)

    qry_blk = split(qry_rows)
    key_blk = split(key_vecs[0])
    val_blk = split(value_vecs[0])
    kv_block = ein("bshe,bshf->bhef", key_blk, val_blk)
    local_kv = jnp.sum(kv_block, 0)
    grad_full = lax.dot_general(
        flat_grad,
        lax.all_gather(out_weight, ("ctx", "dp"), axis=0, tiled=True),
        (((1,), (1,)), ((), ())),
        preferred_element_type=jnp.float32,
    )
    att_grad = grad_full.astype(jnp.bfloat16)
    grd_blk = split(att_grad)
    qd_block = ein("bthf,bthe->bhfe", grd_blk, qry_blk)
    local_qd = jnp.sum(qd_block, 0)
    rows_each = heads_n * HEAD // n_ctx
    kv_parts, qd_parts = (
        lax.all_to_all(
            local_kv.reshape(n_ctx, rows_each, HEAD), "ctx", split_axis=0, concat_axis=0, tiled=True
        ),
        lax.all_to_all(
            local_qd.reshape(n_ctx, rows_each, HEAD), "ctx", split_axis=0, concat_axis=0, tiled=True
        ),
    )
    kv_earlier = jnp.cumsum(kv_parts, 0) - kv_parts
    qd_later = jnp.cumsum(qd_parts[::-1], 0)[::-1] - qd_parts
    kv_back, qd_back = (
        lax.all_to_all(kv_earlier, "ctx", split_axis=0, concat_axis=0, tiled=True),
        lax.all_to_all(qd_later, "ctx", split_axis=0, concat_axis=0, tiled=True),
    )
    kv_before = kv_back.reshape(local_kv.shape)
    qd_after = qd_back.reshape(local_qd.shape)
    state_in = (kv_before[None] + jnp.cumsum(kv_block, 0) - kv_block).astype(jnp.bfloat16)
    carried = (qd_after[None] + jnp.cumsum(qd_block[::-1], 0)[::-1] - qd_block).astype(jnp.bfloat16)
    positions = jnp.arange(BLOCK)
    causal = positions[:, None] >= positions[None, :]
    scores = jnp.where(causal, ein("bthe,bshe->bhts", qry_blk, key_blk), 0.0).astype(jnp.bfloat16)
    attended = att_scale * (
        ein("bhts,bshf->bthf", scores, val_blk) + ein("bthe,bhef->bthf", qry_blk, state_in)
    )
    attended = attended.astype(jnp.bfloat16).reshape(tok_count, width)
    weight_grad = lax.psum_scatter(
        lax.dot_general(
            attended, flat_grad, (((0,), (0,)), ((), ())), preferred_element_type=jnp.float32
        )
        * inv_root,
        ("ctx", "dp"),
        scatter_dimension=0,
        tiled=True,
    )
    dscores = jnp.where(causal, ein("bthf,bshf->bhts", grd_blk, val_blk), 0.0).astype(jnp.bfloat16)
    query_grad = att_scale * (
        ein("bhts,bshe->bthe", dscores, key_blk) + ein("bthf,bhef->bthe", grd_blk, state_in)
    )
    key_grad = att_scale * (
        ein("bhts,bthe->bshe", dscores, qry_blk) + ein("bshf,bhfe->bshe", val_blk, carried)
    )
    value_grad = att_scale * (
        ein("bhts,bthf->bshf", scores, grd_blk) + ein("bshe,bhfe->bshf", key_blk, carried)
    )
    shape_out = (1, tok_count, width)
    return (
        query_grad.astype(jnp.bfloat16).reshape(shape_out),
        key_grad.astype(jnp.bfloat16).reshape(shape_out),
        value_grad.astype(jnp.bfloat16).reshape(shape_out),
        weight_grad,
    )


def solution(mesh):
    placed = (
        P("dp", "ctx", None),
        P("dp", "ctx", None),
        P("dp", "ctx", None),
        P("dp", "ctx", None),
        P(("ctx", "dp"), None),
    )
    n_ctx, n_dp = mesh.shape["ctx"], mesh.shape["dp"]

    def chosen(queries, key_vecs, value_vecs, out_grad, out_weight):
        local = (queries, key_vecs, value_vecs, out_grad, out_weight)
        one_head = out_weight.shape[0] * n_dp == HEAD and n_ctx == 2 * GROUPS
        if one_head and n_dp in (2, 4, 8) and queries.shape[:2] == (1, BLOCK):
            return per_device(n_ctx, n_dp, *local)
        return general_per_device(*local)

    return jax.shard_map(
        chosen,
        mesh=mesh,
        in_specs=placed,
        out_specs=(
            P("dp", "ctx", None),
            P("dp", "ctx", None),
            P("dp", "ctx", None),
            P(("ctx", "dp"), None),
        ),
        check_vma=False,
    )
```

```python
import functools
import math

import jax
import jax.numpy as jnp
from jax import lax
from jax.experimental import pallas as pl
from jax.experimental.pallas import tpu as pltpu
from jax.sharding import PartitionSpec as P

HEAD = 128
BLOCK = 256
GROUPS = 4
BF = jnp.bfloat16
F32 = jnp.float32


def ein(form, left, right):
    return jnp.einsum(form, left, right, preferred_element_type=jnp.float32)


def nn(a, b):
    return lax.dot_general(a, b, (((1,), (0,)), ((), ())), preferred_element_type=F32)


def nt(a, b):
    return lax.dot_general(a, b, (((1,), (1,)), ((), ())), preferred_element_type=F32)


def tn(a, b):
    return lax.dot_general(a, b, (((0,), (0,)), ((), ())), preferred_element_type=F32)


def cols(index):
    return pl.ds(pl.multiple_of(index * HEAD, HEAD), HEAD)


def causal_mask():
    t = lax.broadcasted_iota(jnp.int32, (BLOCK, BLOCK), 0)
    s = lax.broadcasted_iota(jnp.int32, (BLOCK, BLOCK), 1)
    return t >= s, s >= t


def place():
    me = lax.axis_index("ctx")
    return lax.rem(me, 2), lax.div(me, 2)


def local_call(kernel, outs, *args, after=(), scratch=(), streamed=0, aliases=None, micros=0.0):
    vmem = pl.BlockSpec(memory_space=pltpu.VMEM)
    anywhere = pl.BlockSpec(memory_space=pl.ANY)
    count = len(args)

    def body(*refs):
        kernel(*refs[:count], *refs[count + len(after) :])

    return pl.pallas_call(
        body,
        out_shape=[jax.ShapeDtypeStruct(s, d) for s, d in outs],
        in_specs=[vmem] * count + [anywhere] * len(after),
        out_specs=[anywhere] * streamed + [vmem] * (len(outs) - streamed),
        scratch_shapes=scratch,
        input_output_aliases=aliases or {},
        compiler_params=pltpu.CompilerParams(vmem_limit_bytes=24 << 20),
        cost_estimate=pl.CostEstimate(
            flops=int(micros * 1e9), bytes_accessed=int(micros * 3.6e6), transcendentals=0
        ),
    )(*args, *after)


def kv_kernel(kv_o, k_r, v_r, kvsel, psum_sent):
    par, _ = place()
    later = par.astype(F32)
    for j in range(GROUPS):
        c = cols(2 * j + par)
        own = tn(kv_o[0, :, c], kv_o[1, :, c])
        other = tn(k_r[:, c], v_r[:, c])
        kvsel[j] = other * later + own * (1.0 - later)
        psum_sent[j] = (own + other).astype(BF)


def intra_kernel(q_o, kv_o, q_r, k_r, v_r, intra):
    par, _ = place()
    mask, _ = causal_mask()
    kv_both = ((kv_o.at[0], kv_o.at[1]), (k_r, v_r))
    for i, (q, (k, v)) in enumerate(zip((q_o, q_r), kv_both)):
        for j in range(GROUPS):
            c = cols(2 * j + par)
            scores = jnp.where(mask, nt(q[:, c], k[:, c]), 0.0).astype(BF)
            intra[i, :, j * HEAD : (j + 1) * HEAD] = nn(scores, v[:, c])


def attend_kernel(
    att_scale, inv_root, q_o, q_r, g_o, g_r, intra, kvsel, kv_x, kv_y, kv_d,
    to_x, to_y, keep, forward, state_o, state_r,
):
    par, chip = place()
    later = par.astype(F32)
    x_later = lax.rem(chip, 2).astype(F32)
    y_later = lax.div(chip, 2).astype(F32)
    half = g_o.shape[1] // 2
    for m in (3, 1, 2, 0):
        j = lax.bitwise_xor(chip, m)
        earlier = kv_x[j].astype(F32) * x_later
        earlier += (kv_y[j].astype(F32) + kv_d[j].astype(F32)) * y_later
        sel = kvsel[j]
        s_o = (earlier + later * sel).astype(BF)
        s_r = (earlier + (1.0 - later) * sel).astype(BF)
        state_o[j] = s_o
        state_r[j] = s_r
        c = cols(2 * j + par)
        a_o = (att_scale * (intra[0, :, cols(j)] + nn(q_o[:, c], s_o))).astype(BF)
        a_r = (att_scale * (intra[1, :, cols(j)] + nn(q_r[:, c], s_r))).astype(BF)
        term = (tn(a_o, g_o[...]) + tn(a_r, g_r[...])) * inv_root
        first, second = term[:, :half], term[:, half:]
        if m == 3:
            to_x[1], to_y[1] = first.astype(BF), second.astype(BF)
        elif m == 1:
            to_x[0], forward[1] = first.astype(BF), second
        elif m == 2:
            forward[0], to_y[0] = first, second.astype(BF)
        else:
            keep[...] = term


def forward_kernel(side, forward, received, total):
    total[...] = (forward[side] + received[1].astype(F32)).astype(BF)


def fold_kernel(n_dp, keep, from_x, from_y, last_y, last_x, own, *send):
    rows = own.shape[0]
    half = keep.shape[1] // 2
    d = lax.axis_index("dp")
    for m in range(n_dp):
        at = pl.ds(pl.multiple_of(lax.bitwise_xor(d, m) * rows, rows), rows)
        for side, (one, two) in enumerate(((from_x, last_y), (from_y, last_x))):
            c = slice(side * half, (side + 1) * half)
            total = keep[at, c] + one[0, at, :].astype(F32) + two[at, :].astype(F32)
            if m == 0:
                own[:, c] = total
            else:
                send[m - 1][:, c] = total.astype(BF)


def sum_kernel(own, *rest):
    parts, total = rest[:-1], rest[-1]
    total[...] = own[...] + sum(part[...].astype(F32) for part in parts)


def order_kernel(n_dp, *refs):
    parts, full = refs[:-1], refs[-1]
    rows = parts[0].shape[0]
    d = lax.axis_index("dp")
    for m, part in enumerate(parts):
        at = pl.multiple_of(lax.bitwise_xor(d, m) * rows, rows)
        full[pl.ds(at, rows), :] = part[...]


def head_grad(m, at, weights, q_o, q_r, g_o, g_r, ag_o, ag_r, qdsel, psum_sent):
    par, chip = place()
    later = par.astype(F32)
    j = lax.bitwise_xor(chip, m)
    c = cols(2 * j + par)
    a_o, a_r = (
        jnp.concatenate([nt(g[...], w[...]) for w in weights], axis=1).astype(BF)
        for g in (g_o, g_r)
    )
    ag_o[:, at * HEAD : (at + 1) * HEAD] = a_o
    ag_r[:, at * HEAD : (at + 1) * HEAD] = a_r
    own = tn(a_o, q_o[:, c])
    other = tn(a_r, q_r[:, c])
    qdsel[j] = own * later + other * (1.0 - later)
    psum_sent[j] = (own + other).astype(BF)


def near_grad_kernel(q_o, q_r, g_o, g_r, w_0, w_x, w_y, *outs):
    for m, weight in enumerate((w_0, w_x, w_y)):
        head_grad(m, m, (weight,), q_o, q_r, g_o, g_r, *outs)


def far_grad_kernel(
    q_o, q_r, g_o, g_r, w_d0, w_d1, near_sel, near_sent, ag_o, ag_r, qdsel, psum_sent
):
    qdsel[...] = near_sel[...]
    psum_sent[...] = near_sent[...]
    head_grad(3, 0, (w_d0, w_d1), q_o, q_r, g_o, g_r, ag_o, ag_r, qdsel, psum_sent)


def head_block(att_scale, q, k, v, a, state):
    mask, mask_t = causal_mask()
    dscores = jnp.where(mask, nt(a, v), 0.0).astype(BF)
    dscores_t = jnp.where(mask_t, nt(v, a), 0.0).astype(BF)
    scores_t = jnp.where(mask_t, nt(k, q), 0.0).astype(BF)
    dq = (att_scale * (nn(dscores, k) + nt(a, state))).astype(BF)
    return dq, nn(dscores_t, q), nn(scores_t, a)


def near_block_kernel(att_scale, q_o, kv_o, near_o, st_o, dq, dk_in, dv_in):
    par, chip = place()
    for m in range(GROUPS - 1):
        j = lax.bitwise_xor(chip, m)
        c, at = cols(2 * j + par), slice(m * HEAD, (m + 1) * HEAD)
        dq[:, at], dk_in[:, at], dv_in[:, at] = head_block(
            att_scale, q_o[:, c], kv_o[0, :, c], kv_o[1, :, c], near_o[:, at], st_o[j]
        )


def block_kernel(
    att_scale, q_o, kv_o, far_o, near_p, far_p, st_o, st_p, *rest
):
    done, outs = rest[:3], rest[3:]
    par, chip = place()
    for m in range(GROUPS - 1):
        c = cols(2 * lax.bitwise_xor(chip, m) + par)
        for src, dst in zip(done, outs):
            dst[:, c] = src[:, m * HEAD : (m + 1) * HEAD]
    heads = [(par, GROUPS - 1, far_o[...], st_o)]
    for m in range(GROUPS):
        a = near_p[:, m * HEAD : (m + 1) * HEAD] if m < GROUPS - 1 else far_p[...]
        heads.append((1 - par, m, a, st_p))
    for parity, m, a, st in heads:
        j = lax.bitwise_xor(chip, m)
        c = cols(2 * j + parity)
        results = head_block(att_scale, q_o[:, c], kv_o[0, :, c], kv_o[1, :, c], a, st[j])
        for dst, result in zip(outs, results):
            dst[:, c] = result


def carried_kernel(qdsel, qd_x, qd_y, qd_d, car_o, car_r):
    par, chip = place()
    later = par.astype(F32)
    x_earlier = (1 - lax.rem(chip, 2)).astype(F32)
    y_earlier = (1 - lax.div(chip, 2)).astype(F32)
    for j in range(GROUPS):
        total = qd_x[j].astype(F32) * x_earlier
        total += (qd_y[j].astype(F32) + qd_d[j].astype(F32)) * y_earlier
        sel = qdsel[j]
        car_o[j] = (total + (1.0 - later) * sel).astype(BF)
        car_r[j] = (total + later * sel).astype(BF)


def finish_kernel(att_scale, other, kv_o, car, dk_in, dv_in, *refs):
    before, (dk, dv, last, dk_here, dv_here, sems) = refs[:-6], refs[-6:]
    par, _ = place()
    parity = 1 - par if other else par
    copies = []
    if other:
        copies.append(pltpu.make_async_copy(before[0], last, sems.at[2 * GROUPS]))
        copies[0].start()
    else:
        last[...] = jnp.zeros_like(last)
    for j in range(GROUPS):
        c, at = cols(2 * j + parity), slice(j * HEAD, (j + 1) * HEAD)
        carried = car[j]
        dk_here[:, at] = (att_scale * (dk_in[:, c] + nn(kv_o[1, :, c], carried))).astype(BF)
        dv_here[:, at] = (att_scale * (dv_in[:, c] + nt(kv_o[0, :, c], carried))).astype(BF)
        for here, out in ((dk_here, dk), (dv_here, dv)):
            sem = sems.at[len(copies) - other]
            copies.append(pltpu.make_async_copy(here.at[:, at], out.at[:, c], sem))
            copies[-1].start()
    for copy in copies:
        copy.wait()


def per_device(n_ctx, n_dp, queries, key_vecs, value_vecs, out_grad, out_weight):
    tok_count, width = queries.shape[1:]
    att_scale = 1.0 / math.sqrt(HEAD * tok_count * n_ctx)
    inv_root = 1.0 / math.sqrt(n_dp * tok_count * n_ctx)

    def along(bit):
        return [(i, i ^ bit) for i in range(n_ctx)]

    def core(x):
        return lax.ppermute(x, "ctx", along(1))

    def over_x(x):
        return lax.ppermute(x, "ctx", along(2))

    def over_y(x):
        return lax.ppermute(x, "ctx", along(4))

    def over_both(x):
        return lax.ppermute(x, "ctx", along(6))

    def along_dp(x, m):
        return lax.ppermute(x, "dp", [(i, i ^ m) for i in range(n_dp)])

    state = (GROUPS, HEAD, HEAD)
    half = width // 2
    rows = HEAD // n_dp
    q_o, k_o, v_o, g_o = queries[0], key_vecs[0], value_vecs[0], out_grad[0]
    k_r, v_r, q_r, g_r = core(k_o), core(v_o), core(q_o), core(g_o)
    kv_o = jnp.concatenate([key_vecs, value_vecs])
    w_parts = [along_dp(out_weight, m) for m in range(1, n_dp)]
    kvsel, kv_sent = local_call(
        kv_kernel,
        [(state, F32), (state, BF)],
        kv_o, k_r, v_r,
        after=(q_r, g_r),
    )
    kv_x, kv_y, kv_d = over_x(kv_sent), over_y(kv_sent), over_both(kv_sent)
    (w_0,) = local_call(
        functools.partial(order_kernel, n_dp),
        [((HEAD, width), BF)], out_weight, *w_parts, after=(kv_sent,), micros=20,
    )
    (intra,) = local_call(
        intra_kernel,
        [((2, BLOCK, half), F32)], q_o, kv_o, q_r, k_r, v_r, after=(w_0,),
    )
    w_x, w_y = over_x(w_0), over_y(w_0)
    w_d0, w_d1 = over_y(w_x[: HEAD // 2]), over_x(w_y[HEAD // 2 :])
    to_x, to_y, keep, forward, state_o, state_r = local_call(
        functools.partial(attend_kernel, att_scale, inv_root),
        [
            ((2, HEAD, half), BF),
            ((2, HEAD, half), BF),
            ((HEAD, width), F32),
            ((2, HEAD, half), F32),
            (state, BF),
            (state, BF),
        ],
        q_o, q_r, g_o, g_r, intra, kvsel, kv_x, kv_y, kv_d,
    )
    from_x, from_y = over_x(to_x), over_y(to_y)
    state_p = core(state_r)
    sums = [(state, F32), (state, BF)]
    near_o, near_r, near_sel, near_sent = local_call(
        near_grad_kernel,
        [((BLOCK, half - HEAD), BF)] * 2 + sums,
        q_o, q_r, g_o, g_r, w_0, w_x, w_y,
        after=(state_p,),
    )
    near_p = core(near_r)
    near_done = local_call(
        functools.partial(near_block_kernel, att_scale),
        [((BLOCK, half - HEAD), kind) for kind in (BF, F32, F32)],
        q_o, kv_o, near_o, state_o,
    )
    (pass_y,) = local_call(
        functools.partial(forward_kernel, 0), [((HEAD, half), BF)], forward, from_x,
        after=(near_done[0],),
    )
    (pass_x,) = local_call(
        functools.partial(forward_kernel, 1), [((HEAD, half), BF)], forward, from_y,
        after=(pass_y,),
    )
    last_y, last_x = over_y(pass_y), over_x(pass_x)
    far_o, far_r, qdsel, qd_sent = local_call(
        far_grad_kernel,
        [((BLOCK, HEAD), BF)] * 2 + sums,
        q_o, q_r, g_o, g_r, w_d0, w_d1, near_sel, near_sent,
        after=(pass_x,),
    )
    qd_x, qd_y, qd_d = over_x(qd_sent), over_y(qd_sent), over_both(qd_sent)
    far_p = core(far_r)
    own, *send = local_call(
        functools.partial(fold_kernel, n_dp),
        [((rows, width), F32)] + [((rows, width), BF)] * (n_dp - 1),
        keep, from_x, from_y, last_y, last_x,
        after=(far_p, near_p), micros=20,
    )
    got = [along_dp(send[m - 1], m) for m in range(1, n_dp)]
    dq, dk_in, dv_in = local_call(
        functools.partial(block_kernel, att_scale),
        [((BLOCK, width), BF), ((BLOCK, width), F32), ((BLOCK, width), F32)],
        q_o, kv_o, far_o, near_p, far_p, state_o, state_p, *near_done,
        after=(send[0],),
    )
    car_o, car_r = local_call(
        carried_kernel, [(state, BF), (state, BF)], qdsel, qd_x, qd_y, qd_d, after=(dk_in,)
    )
    car_p = core(car_r)
    grads = [((BLOCK, width), BF), ((BLOCK, width), BF)]
    streams = [
        pltpu.VMEM((BLOCK, half), BF),
        pltpu.VMEM((BLOCK, half), BF),
        pltpu.SemaphoreType.DMA((2 * GROUPS + 1,)),
    ]
    dk, dv, ended = local_call(
        functools.partial(finish_kernel, att_scale, 0),
        grads + [((8, HEAD), F32)],
        kv_o, car_o, dk_in, dv_in,
        streamed=2,
        scratch=streams,
    )
    (summed,) = local_call(
        sum_kernel, [((rows, width), F32)], own, *got, after=(ended,), micros=20
    )
    dk, dv, weight_grad = local_call(
        functools.partial(finish_kernel, att_scale, 1),
        grads + [((rows, width), F32)],
        kv_o, car_p, dk_in, dv_in, summed,
        after=(dk, dv),
        aliases={5: 0, 6: 1},
        streamed=3,
        scratch=streams,
    )
    return dq[None], dk[None], dv[None], weight_grad


def general_per_device(queries, key_vecs, value_vecs, out_grad, out_weight):
    qry_rows = queries[0]
    tok_count = qry_rows.shape[0]
    width = qry_rows.shape[1]
    heads_n = width // HEAD
    count = tok_count // BLOCK
    n_ctx = lax.axis_size("ctx")
    n_dp = lax.axis_size("dp")
    att_scale = 1.0 / math.sqrt(HEAD * tok_count * n_ctx)
    inv_root = 1.0 / math.sqrt(n_dp * tok_count * n_ctx)
    flat_grad = out_grad[0]

    def split(array):
        return array.reshape(count, BLOCK, heads_n, HEAD)

    qry_blk = split(qry_rows)
    key_blk = split(key_vecs[0])
    val_blk = split(value_vecs[0])
    kv_block = ein("bshe,bshf->bhef", key_blk, val_blk)
    local_kv = jnp.sum(kv_block, 0)
    grad_full = lax.dot_general(
        flat_grad,
        lax.all_gather(out_weight, ("ctx", "dp"), axis=0, tiled=True),
        (((1,), (1,)), ((), ())),
        preferred_element_type=jnp.float32,
    )
    att_grad = grad_full.astype(jnp.bfloat16)
    grd_blk = split(att_grad)
    qd_block = ein("bthf,bthe->bhfe", grd_blk, qry_blk)
    local_qd = jnp.sum(qd_block, 0)
    rows_each = heads_n * HEAD // n_ctx
    kv_parts, qd_parts = (
        lax.all_to_all(
            local_kv.reshape(n_ctx, rows_each, HEAD), "ctx", split_axis=0, concat_axis=0, tiled=True
        ),
        lax.all_to_all(
            local_qd.reshape(n_ctx, rows_each, HEAD), "ctx", split_axis=0, concat_axis=0, tiled=True
        ),
    )
    kv_earlier = jnp.cumsum(kv_parts, 0) - kv_parts
    qd_later = jnp.cumsum(qd_parts[::-1], 0)[::-1] - qd_parts
    kv_back, qd_back = (
        lax.all_to_all(kv_earlier, "ctx", split_axis=0, concat_axis=0, tiled=True),
        lax.all_to_all(qd_later, "ctx", split_axis=0, concat_axis=0, tiled=True),
    )
    kv_before = kv_back.reshape(local_kv.shape)
    qd_after = qd_back.reshape(local_qd.shape)
    state_in = (kv_before[None] + jnp.cumsum(kv_block, 0) - kv_block).astype(jnp.bfloat16)
    carried = (qd_after[None] + jnp.cumsum(qd_block[::-1], 0)[::-1] - qd_block).astype(jnp.bfloat16)
    positions = jnp.arange(BLOCK)
    causal = positions[:, None] >= positions[None, :]
    scores = jnp.where(causal, ein("bthe,bshe->bhts", qry_blk, key_blk), 0.0).astype(jnp.bfloat16)
    attended = att_scale * (
        ein("bhts,bshf->bthf", scores, val_blk) + ein("bthe,bhef->bthf", qry_blk, state_in)
    )
    attended = attended.astype(jnp.bfloat16).reshape(tok_count, width)
    weight_grad = lax.psum_scatter(
        lax.dot_general(
            attended, flat_grad, (((0,), (0,)), ((), ())), preferred_element_type=jnp.float32
        )
        * inv_root,
        ("ctx", "dp"),
        scatter_dimension=0,
        tiled=True,
    )
    dscores = jnp.where(causal, ein("bthf,bshf->bhts", grd_blk, val_blk), 0.0).astype(jnp.bfloat16)
    query_grad = att_scale * (
        ein("bhts,bshe->bthe", dscores, key_blk) + ein("bthf,bhef->bthe", grd_blk, state_in)
    )
    key_grad = att_scale * (
        ein("bhts,bthe->bshe", dscores, qry_blk) + ein("bshf,bhfe->bshe", val_blk, carried)
    )
    value_grad = att_scale * (
        ein("bhts,bthf->bshf", scores, grd_blk) + ein("bshe,bhfe->bshf", key_blk, carried)
    )
    shape_out = (1, tok_count, width)
    return (
        query_grad.astype(jnp.bfloat16).reshape(shape_out),
        key_grad.astype(jnp.bfloat16).reshape(shape_out),
        value_grad.astype(jnp.bfloat16).reshape(shape_out),
        weight_grad,
    )


def solution(mesh):
    placed = (
        P("dp", "ctx", None),
        P("dp", "ctx", None),
        P("dp", "ctx", None),
        P("dp", "ctx", None),
        P(("ctx", "dp"), None),
    )
    n_ctx, n_dp = mesh.shape["ctx"], mesh.shape["dp"]

    def chosen(queries, key_vecs, value_vecs, out_grad, out_weight):
        local = (queries, key_vecs, value_vecs, out_grad, out_weight)
        one_head = out_weight.shape[0] * n_dp == HEAD and n_ctx == 2 * GROUPS
        if one_head and n_dp in (2, 4, 8) and queries.shape[:2] == (1, BLOCK):
            return per_device(n_ctx, n_dp, *local)
        return general_per_device(*local)

    return jax.shard_map(
        chosen,
        mesh=mesh,
        in_specs=placed,
        out_specs=(
            P("dp", "ctx", None),
            P("dp", "ctx", None),
            P("dp", "ctx", None),
            P(("ctx", "dp"), None),
        ),
        check_vma=False,
    )
```

```python
import functools
import math

import jax
import jax.numpy as jnp
from jax import lax
from jax.experimental import pallas as pl
from jax.experimental.pallas import tpu as pltpu
from jax.sharding import PartitionSpec as P

HEAD = 128
BLOCK = 256
GROUPS = 4
BF = jnp.bfloat16
F32 = jnp.float32


def ein(form, left, right):
    return jnp.einsum(form, left, right, preferred_element_type=jnp.float32)


def nn(a, b):
    return lax.dot_general(a, b, (((1,), (0,)), ((), ())), preferred_element_type=F32)


def nt(a, b):
    return lax.dot_general(a, b, (((1,), (1,)), ((), ())), preferred_element_type=F32)


def tn(a, b):
    return lax.dot_general(a, b, (((0,), (0,)), ((), ())), preferred_element_type=F32)


def feature_rows(a, b):
    return lax.dot_general(a, b, (((0,), (1,)), ((), ())), preferred_element_type=F32)


def cols(index):
    return pl.ds(pl.multiple_of(index * HEAD, HEAD), HEAD)


def causal_mask():
    t = lax.broadcasted_iota(jnp.int32, (BLOCK, BLOCK), 0)
    s = lax.broadcasted_iota(jnp.int32, (BLOCK, BLOCK), 1)
    return t >= s, s >= t


def place():
    me = lax.axis_index("ctx")
    return lax.rem(me, 2), lax.div(me, 2)


def local_call(kernel, outs, *args, after=(), scratch=(), streamed=0, aliases=None, micros=0.0):
    vmem = pl.BlockSpec(memory_space=pltpu.VMEM)
    anywhere = pl.BlockSpec(memory_space=pl.ANY)
    count = len(args)

    def body(*refs):
        kernel(*refs[:count], *refs[count + len(after) :])

    return pl.pallas_call(
        body,
        out_shape=[jax.ShapeDtypeStruct(s, d) for s, d in outs],
        in_specs=[vmem] * count + [anywhere] * len(after),
        out_specs=[anywhere] * streamed + [vmem] * (len(outs) - streamed),
        scratch_shapes=scratch,
        input_output_aliases=aliases or {},
        compiler_params=pltpu.CompilerParams(vmem_limit_bytes=24 << 20),
        cost_estimate=pl.CostEstimate(
            flops=int(micros * 1e9), bytes_accessed=int(micros * 3.6e6), transcendentals=0
        ),
    )(*args, *after)


def kv_kernel(kv_o, k_r, v_r, kvsel, psum_sent):
    par, _ = place()
    later = par.astype(F32)
    for j in range(GROUPS):
        c = cols(2 * j + par)
        own = tn(kv_o[0, :, c], kv_o[1, :, c])
        other = tn(k_r[:, c], v_r[:, c])
        kvsel[j] = other * later + own * (1.0 - later)
        psum_sent[j] = (own + other).astype(BF)


def intra_kernel(q_o, kv_o, q_r, k_r, v_r, intra):
    par, _ = place()
    mask, _ = causal_mask()
    kv_both = ((kv_o.at[0], kv_o.at[1]), (k_r, v_r))
    for i, (q, (k, v)) in enumerate(zip((q_o, q_r), kv_both)):
        for j in range(GROUPS):
            c = cols(2 * j + par)
            scores = jnp.where(mask, nt(q[:, c], k[:, c]), 0.0).astype(BF)
            intra[i, j * HEAD : (j + 1) * HEAD, :] = feature_rows(v[:, c], scores)


def attend_kernel(
    att_scale, inv_root, q_o, q_r, g_o, g_r, intra, kvsel, kv_x, kv_y, kv_d,
    to_x, to_y, keep, forward, state_o, state_r,
):
    par, chip = place()
    later = par.astype(F32)
    x_later = lax.rem(chip, 2).astype(F32)
    y_later = lax.div(chip, 2).astype(F32)
    half = g_o.shape[1] // 2
    for m in (3, 1, 2, 0):
        j = lax.bitwise_xor(chip, m)
        earlier = kv_x[j].astype(F32) * x_later
        earlier += (kv_y[j].astype(F32) + kv_d[j].astype(F32)) * y_later
        sel = kvsel[j]
        s_o = (earlier + later * sel).astype(BF)
        s_r = (earlier + (1.0 - later) * sel).astype(BF)
        state_o[j] = s_o
        state_r[j] = s_r
        c = cols(2 * j + par)
        a_o = (att_scale * (intra[0, cols(j), :] + feature_rows(s_o, q_o[:, c]))).astype(BF)
        a_r = (att_scale * (intra[1, cols(j), :] + feature_rows(s_r, q_r[:, c]))).astype(BF)
        term = (nn(a_o, g_o[...]) + nn(a_r, g_r[...])) * inv_root
        first, second = term[:, :half], term[:, half:]
        if m == 3:
            to_x[1], to_y[1] = first.astype(BF), second.astype(BF)
        elif m == 1:
            to_x[0], forward[1] = first.astype(BF), second
        elif m == 2:
            forward[0], to_y[0] = first, second.astype(BF)
        else:
            keep[...] = term


def forward_kernel(side, forward, received, total):
    total[...] = (forward[side] + received[1].astype(F32)).astype(BF)


def fold_kernel(n_dp, keep, from_x, from_y, last_y, last_x, own, *send):
    rows = own.shape[0]
    half = keep.shape[1] // 2
    d = lax.axis_index("dp")
    for m in range(n_dp):
        at = pl.ds(pl.multiple_of(lax.bitwise_xor(d, m) * rows, rows), rows)
        for side, (one, two) in enumerate(((from_x, last_y), (from_y, last_x))):
            c = slice(side * half, (side + 1) * half)
            total = keep[at, c] + one[0, at, :].astype(F32) + two[at, :].astype(F32)
            if m == 0:
                own[:, c] = total
            else:
                send[m - 1][:, c] = total.astype(BF)


def sum_kernel(own, *rest):
    parts, total = rest[:-1], rest[-1]
    total[...] = own[...] + sum(part[...].astype(F32) for part in parts)


def order_kernel(n_dp, *refs):
    parts, full = refs[:-1], refs[-1]
    rows = parts[0].shape[0]
    d = lax.axis_index("dp")
    for m, part in enumerate(parts):
        at = pl.multiple_of(lax.bitwise_xor(d, m) * rows, rows)
        full[pl.ds(at, rows), :] = part[...]


def head_grad(m, at, weights, q_o, q_r, g_o, g_r, ag_o, ag_r, qdsel, psum_sent):
    par, chip = place()
    later = par.astype(F32)
    j = lax.bitwise_xor(chip, m)
    c = cols(2 * j + par)
    a_o, a_r = (
        jnp.concatenate([nt(g[...], w[...]) for w in weights], axis=1).astype(BF)
        for g in (g_o, g_r)
    )
    ag_o[:, at * HEAD : (at + 1) * HEAD] = a_o
    ag_r[:, at * HEAD : (at + 1) * HEAD] = a_r
    own = tn(a_o, q_o[:, c])
    other = tn(a_r, q_r[:, c])
    qdsel[j] = own * later + other * (1.0 - later)
    psum_sent[j] = (own + other).astype(BF)


def near_grad_kernel(q_o, q_r, g_o, g_r, w_0, w_x, w_y, *outs):
    for m, weight in enumerate((w_0, w_x, w_y)):
        head_grad(m, m, (weight,), q_o, q_r, g_o, g_r, *outs)


def far_grad_kernel(
    q_o, q_r, g_o, g_r, w_d0, w_d1, near_sel, near_sent, ag_o, ag_r, qdsel, psum_sent
):
    qdsel[...] = near_sel[...]
    psum_sent[...] = near_sent[...]
    head_grad(3, 0, (w_d0, w_d1), q_o, q_r, g_o, g_r, ag_o, ag_r, qdsel, psum_sent)


def head_block(att_scale, q, k, v, a, state):
    mask, mask_t = causal_mask()
    dscores = jnp.where(mask, nt(a, v), 0.0).astype(BF)
    dscores_t = jnp.where(mask_t, nt(v, a), 0.0).astype(BF)
    scores_t = jnp.where(mask_t, nt(k, q), 0.0).astype(BF)
    dq = (att_scale * (nn(dscores, k) + nt(a, state))).astype(BF)
    return dq, nn(dscores_t, q), nn(scores_t, a)


def near_block_kernel(att_scale, q_o, kv_o, near_o, st_o, dq, dk_in, dv_in):
    par, chip = place()
    for m in range(GROUPS - 1):
        j = lax.bitwise_xor(chip, m)
        c, at = cols(2 * j + par), slice(m * HEAD, (m + 1) * HEAD)
        dq[:, at], dk_in[:, at], dv_in[:, at] = head_block(
            att_scale, q_o[:, c], kv_o[0, :, c], kv_o[1, :, c], near_o[:, at], st_o[j]
        )


def block_kernel(
    att_scale, q_o, kv_o, far_o, near_p, far_p, st_o, st_p, *rest
):
    done, outs = rest[:3], rest[3:]
    par, chip = place()
    for m in range(GROUPS - 1):
        c = cols(2 * lax.bitwise_xor(chip, m) + par)
        for src, dst in zip(done, outs):
            dst[:, c] = src[:, m * HEAD : (m + 1) * HEAD]
    heads = [(par, GROUPS - 1, far_o[...], st_o)]
    for m in range(GROUPS):
        a = near_p[:, m * HEAD : (m + 1) * HEAD] if m < GROUPS - 1 else far_p[...]
        heads.append((1 - par, m, a, st_p))
    for parity, m, a, st in heads:
        j = lax.bitwise_xor(chip, m)
        c = cols(2 * j + parity)
        results = head_block(att_scale, q_o[:, c], kv_o[0, :, c], kv_o[1, :, c], a, st[j])
        for dst, result in zip(outs, results):
            dst[:, c] = result


def carried_kernel(qdsel, qd_x, qd_y, qd_d, car_o, car_r):
    par, chip = place()
    later = par.astype(F32)
    x_earlier = (1 - lax.rem(chip, 2)).astype(F32)
    y_earlier = (1 - lax.div(chip, 2)).astype(F32)
    for j in range(GROUPS):
        total = qd_x[j].astype(F32) * x_earlier
        total += (qd_y[j].astype(F32) + qd_d[j].astype(F32)) * y_earlier
        sel = qdsel[j]
        car_o[j] = (total + (1.0 - later) * sel).astype(BF)
        car_r[j] = (total + later * sel).astype(BF)


def finish_kernel(att_scale, other, kv_o, car, dk_in, dv_in, *refs):
    before, (dk, dv, last, dk_here, dv_here, sems) = refs[:-6], refs[-6:]
    par, _ = place()
    parity = 1 - par if other else par
    copies = []
    if other:
        copies.append(pltpu.make_async_copy(before[0], last, sems.at[2 * GROUPS]))
        copies[0].start()
    else:
        last[...] = jnp.zeros_like(last)
    for j in range(GROUPS):
        c, at = cols(2 * j + parity), slice(j * HEAD, (j + 1) * HEAD)
        carried = car[j]
        dk_here[:, at] = (att_scale * (dk_in[:, c] + nn(kv_o[1, :, c], carried))).astype(BF)
        dv_here[:, at] = (att_scale * (dv_in[:, c] + nt(kv_o[0, :, c], carried))).astype(BF)
        for here, out in ((dk_here, dk), (dv_here, dv)):
            sem = sems.at[len(copies) - other]
            copies.append(pltpu.make_async_copy(here.at[:, at], out.at[:, c], sem))
            copies[-1].start()
    for copy in copies:
        copy.wait()


def per_device(n_ctx, n_dp, queries, key_vecs, value_vecs, out_grad, out_weight):
    tok_count, width = queries.shape[1:]
    att_scale = 1.0 / math.sqrt(HEAD * tok_count * n_ctx)
    inv_root = 1.0 / math.sqrt(n_dp * tok_count * n_ctx)

    def along(bit):
        return [(i, i ^ bit) for i in range(n_ctx)]

    def core(x):
        return lax.ppermute(x, "ctx", along(1))

    def over_x(x):
        return lax.ppermute(x, "ctx", along(2))

    def over_y(x):
        return lax.ppermute(x, "ctx", along(4))

    def over_both(x):
        return lax.ppermute(x, "ctx", along(6))

    def along_dp(x, m):
        return lax.ppermute(x, "dp", [(i, i ^ m) for i in range(n_dp)])

    state = (GROUPS, HEAD, HEAD)
    half = width // 2
    rows = HEAD // n_dp
    q_o, k_o, v_o, g_o = queries[0], key_vecs[0], value_vecs[0], out_grad[0]
    k_r, v_r, q_r, g_r = core(k_o), core(v_o), core(q_o), core(g_o)
    kv_o = jnp.concatenate([key_vecs, value_vecs])
    w_parts = [along_dp(out_weight, m) for m in range(1, n_dp)]
    kvsel, kv_sent = local_call(
        kv_kernel,
        [(state, F32), (state, BF)],
        kv_o, k_r, v_r,
        after=(q_r, g_r),
    )
    kv_x, kv_y, kv_d = over_x(kv_sent), over_y(kv_sent), over_both(kv_sent)
    (w_0,) = local_call(
        functools.partial(order_kernel, n_dp),
        [((HEAD, width), BF)], out_weight, *w_parts, after=(kv_sent,), micros=20,
    )
    (intra,) = local_call(
        intra_kernel,
        [((2, half, BLOCK), F32)], q_o, kv_o, q_r, k_r, v_r, after=(w_0,),
    )
    w_x, w_y = over_x(w_0), over_y(w_0)
    w_d0, w_d1 = over_y(w_x[: HEAD // 2]), over_x(w_y[HEAD // 2 :])
    to_x, to_y, keep, forward, state_o, state_r = local_call(
        functools.partial(attend_kernel, att_scale, inv_root),
        [
            ((2, HEAD, half), BF),
            ((2, HEAD, half), BF),
            ((HEAD, width), F32),
            ((2, HEAD, half), F32),
            (state, BF),
            (state, BF),
        ],
        q_o, q_r, g_o, g_r, intra, kvsel, kv_x, kv_y, kv_d,
    )
    from_x, from_y = over_x(to_x), over_y(to_y)
    state_p = core(state_r)
    sums = [(state, F32), (state, BF)]
    near_o, near_r, near_sel, near_sent = local_call(
        near_grad_kernel,
        [((BLOCK, half - HEAD), BF)] * 2 + sums,
        q_o, q_r, g_o, g_r, w_0, w_x, w_y,
        after=(state_p,),
    )
    near_p = core(near_r)
    near_done = local_call(
        functools.partial(near_block_kernel, att_scale),
        [((BLOCK, half - HEAD), kind) for kind in (BF, F32, F32)],
        q_o, kv_o, near_o, state_o,
    )
    (pass_y,) = local_call(
        functools.partial(forward_kernel, 0), [((HEAD, half), BF)], forward, from_x,
        after=(near_done[0],),
    )
    (pass_x,) = local_call(
        functools.partial(forward_kernel, 1), [((HEAD, half), BF)], forward, from_y,
        after=(pass_y,),
    )
    last_y, last_x = over_y(pass_y), over_x(pass_x)
    far_o, far_r, qdsel, qd_sent = local_call(
        far_grad_kernel,
        [((BLOCK, HEAD), BF)] * 2 + sums,
        q_o, q_r, g_o, g_r, w_d0, w_d1, near_sel, near_sent,
        after=(pass_x,),
    )
    qd_x, qd_y, qd_d = over_x(qd_sent), over_y(qd_sent), over_both(qd_sent)
    far_p = core(far_r)
    own, *send = local_call(
        functools.partial(fold_kernel, n_dp),
        [((rows, width), F32)] + [((rows, width), BF)] * (n_dp - 1),
        keep, from_x, from_y, last_y, last_x,
        after=(far_p, near_p), micros=20,
    )
    got = [along_dp(send[m - 1], m) for m in range(1, n_dp)]
    dq, dk_in, dv_in = local_call(
        functools.partial(block_kernel, att_scale),
        [((BLOCK, width), BF), ((BLOCK, width), F32), ((BLOCK, width), F32)],
        q_o, kv_o, far_o, near_p, far_p, state_o, state_p, *near_done,
        after=(send[0],),
    )
    car_o, car_r = local_call(
        carried_kernel, [(state, BF), (state, BF)], qdsel, qd_x, qd_y, qd_d, after=(dk_in,)
    )
    car_p = core(car_r)
    grads = [((BLOCK, width), BF), ((BLOCK, width), BF)]
    streams = [
        pltpu.VMEM((BLOCK, half), BF),
        pltpu.VMEM((BLOCK, half), BF),
        pltpu.SemaphoreType.DMA((2 * GROUPS + 1,)),
    ]
    dk, dv, ended = local_call(
        functools.partial(finish_kernel, att_scale, 0),
        grads + [((8, HEAD), F32)],
        kv_o, car_o, dk_in, dv_in,
        streamed=2,
        scratch=streams,
    )
    (summed,) = local_call(
        sum_kernel, [((rows, width), F32)], own, *got, after=(ended,), micros=20
    )
    dk, dv, weight_grad = local_call(
        functools.partial(finish_kernel, att_scale, 1),
        grads + [((rows, width), F32)],
        kv_o, car_p, dk_in, dv_in, summed,
        after=(dk, dv),
        aliases={5: 0, 6: 1},
        streamed=3,
        scratch=streams,
    )
    return dq[None], dk[None], dv[None], weight_grad


def general_per_device(queries, key_vecs, value_vecs, out_grad, out_weight):
    qry_rows = queries[0]
    tok_count = qry_rows.shape[0]
    width = qry_rows.shape[1]
    heads_n = width // HEAD
    count = tok_count // BLOCK
    n_ctx = lax.axis_size("ctx")
    n_dp = lax.axis_size("dp")
    att_scale = 1.0 / math.sqrt(HEAD * tok_count * n_ctx)
    inv_root = 1.0 / math.sqrt(n_dp * tok_count * n_ctx)
    flat_grad = out_grad[0]

    def split(array):
        return array.reshape(count, BLOCK, heads_n, HEAD)

    qry_blk = split(qry_rows)
    key_blk = split(key_vecs[0])
    val_blk = split(value_vecs[0])
    kv_block = ein("bshe,bshf->bhef", key_blk, val_blk)
    local_kv = jnp.sum(kv_block, 0)
    grad_full = lax.dot_general(
        flat_grad,
        lax.all_gather(out_weight, ("ctx", "dp"), axis=0, tiled=True),
        (((1,), (1,)), ((), ())),
        preferred_element_type=jnp.float32,
    )
    att_grad = grad_full.astype(jnp.bfloat16)
    grd_blk = split(att_grad)
    qd_block = ein("bthf,bthe->bhfe", grd_blk, qry_blk)
    local_qd = jnp.sum(qd_block, 0)
    rows_each = heads_n * HEAD // n_ctx
    kv_parts, qd_parts = (
        lax.all_to_all(
            local_kv.reshape(n_ctx, rows_each, HEAD), "ctx", split_axis=0, concat_axis=0, tiled=True
        ),
        lax.all_to_all(
            local_qd.reshape(n_ctx, rows_each, HEAD), "ctx", split_axis=0, concat_axis=0, tiled=True
        ),
    )
    kv_earlier = jnp.cumsum(kv_parts, 0) - kv_parts
    qd_later = jnp.cumsum(qd_parts[::-1], 0)[::-1] - qd_parts
    kv_back, qd_back = (
        lax.all_to_all(kv_earlier, "ctx", split_axis=0, concat_axis=0, tiled=True),
        lax.all_to_all(qd_later, "ctx", split_axis=0, concat_axis=0, tiled=True),
    )
    kv_before = kv_back.reshape(local_kv.shape)
    qd_after = qd_back.reshape(local_qd.shape)
    state_in = (kv_before[None] + jnp.cumsum(kv_block, 0) - kv_block).astype(jnp.bfloat16)
    carried = (qd_after[None] + jnp.cumsum(qd_block[::-1], 0)[::-1] - qd_block).astype(jnp.bfloat16)
    positions = jnp.arange(BLOCK)
    causal = positions[:, None] >= positions[None, :]
    scores = jnp.where(causal, ein("bthe,bshe->bhts", qry_blk, key_blk), 0.0).astype(jnp.bfloat16)
    attended = att_scale * (
        ein("bhts,bshf->bthf", scores, val_blk) + ein("bthe,bhef->bthf", qry_blk, state_in)
    )
    attended = attended.astype(jnp.bfloat16).reshape(tok_count, width)
    weight_grad = lax.psum_scatter(
        lax.dot_general(
            attended, flat_grad, (((0,), (0,)), ((), ())), preferred_element_type=jnp.float32
        )
        * inv_root,
        ("ctx", "dp"),
        scatter_dimension=0,
        tiled=True,
    )
    dscores = jnp.where(causal, ein("bthf,bshf->bhts", grd_blk, val_blk), 0.0).astype(jnp.bfloat16)
    query_grad = att_scale * (
        ein("bhts,bshe->bthe", dscores, key_blk) + ein("bthf,bhef->bthe", grd_blk, state_in)
    )
    key_grad = att_scale * (
        ein("bhts,bthe->bshe", dscores, qry_blk) + ein("bshf,bhfe->bshe", val_blk, carried)
    )
    value_grad = att_scale * (
        ein("bhts,bthf->bshf", scores, grd_blk) + ein("bshe,bhfe->bshf", key_blk, carried)
    )
    shape_out = (1, tok_count, width)
    return (
        query_grad.astype(jnp.bfloat16).reshape(shape_out),
        key_grad.astype(jnp.bfloat16).reshape(shape_out),
        value_grad.astype(jnp.bfloat16).reshape(shape_out),
        weight_grad,
    )


def solution(mesh):
    placed = (
        P("dp", "ctx", None),
        P("dp", "ctx", None),
        P("dp", "ctx", None),
        P("dp", "ctx", None),
        P(("ctx", "dp"), None),
    )
    n_ctx, n_dp = mesh.shape["ctx"], mesh.shape["dp"]

    def chosen(queries, key_vecs, value_vecs, out_grad, out_weight):
        local = (queries, key_vecs, value_vecs, out_grad, out_weight)
        one_head = out_weight.shape[0] * n_dp == HEAD and n_ctx == 2 * GROUPS
        if one_head and n_dp in (2, 4, 8) and queries.shape[:2] == (1, BLOCK):
            return per_device(n_ctx, n_dp, *local)
        return general_per_device(*local)

    return jax.shard_map(
        chosen,
        mesh=mesh,
        in_specs=placed,
        out_specs=(
            P("dp", "ctx", None),
            P("dp", "ctx", None),
            P("dp", "ctx", None),
            P(("ctx", "dp"), None),
        ),
        check_vma=False,
    )
```
